256 devices in a mesh: patch: 64 (over y, z, core), sample: 4 (over x).
Axes of the slice: x: 4, y: 4, z: 8, core: 2. Of those that a mesh axis runs over, the one named last changes fastest.
Arguments:
- edge_latents: bfloat16 [4, 65536, 512], P('sample', 'patch'), may hold values from -6 to 6
- node_latents: bfloat16 [4, 16384, 512], P('sample', 'patch'), may hold values from -6 to 6
- edge_cotangent: bfloat16 [4, 65536, 512], P('sample', 'patch'), may hold values from -6 to 6
- node_cotangent: bfloat16 [4, 16384, 512], P('sample', 'patch'), may hold values from -6 to 6
- senders: int32 [65536], P('patch'), may hold values from 0 to 575, as said below
- receivers: int32 [65536], P('patch'), may hold values from 0 to 255
- send_rows: int32 [4096, 4], P('patch'), may hold values from 0 to 255
- edge_first: bfloat16 [1536, 512], replicated, may hold values from -0.15625 to 0.15625
- edge_second: bfloat16 [512, 512], replicated, may hold values from -0.25 to 0.25
- edge_gain: float32 [512], replicated, may hold values from 0.25 to 1.75
- node_first: bfloat16 [1024, 512], replicated, may hold values from -0.1875 to 0.1875
- node_second: bfloat16 [512, 512], replicated, may hold values from -0.25 to 0.25
- node_gain: float32 [512], replicated, may hold values from 0.25 to 1.75
Outputs:
- edge_grad: bfloat16 [4, 65536, 512], P('sample', 'patch')
- node_grad: bfloat16 [4, 16384, 512], P('sample', 'patch')
- edge_first_grad: bfloat16 [1536, 512], replicated
- edge_second_grad: bfloat16 [512, 512], replicated
- node_first_grad: bfloat16 [1024, 512], replicated
- node_second_grad: bfloat16 [512, 512], replicated
- edge_gain_grad: bfloat16 [512], replicated
- node_gain_grad: bfloat16 [512], replicated
The draws below stay inside these ranges and needn't reach their ends.
Inputs may be any that keep to these rules, and one draw needn't show every extreme that they name: `senders`: each patch's sender table has 576 rows: the last 32 nodes of the patch before it (cyclically), its own 256 nodes, the first 32 nodes of the patch after it, then 4 rows from each patch in order.
All inputs are finite; a program needn't handle non-finite values.
Results may differ from the reference program's by a relative error of at most 0.012.
Values may be sent and summed in bfloat16 or wider, within the bound.
A program may use at most 128 MiB of HBM per device.

```python
import jax
import jax.numpy as jnp
from jax import lax

D = 512
HID = 512
N_DEV = 256
E_DEV = 1024
RIM = 32
FAR = 4
NODES = 16384
EDGES = 65536
SAMPLES = 4
N_PATCH = 64


def draw_senders(key, part):
    key = jax.random.fold_in(key, 11)
    keys = jax.random.split(key, 6)
    kinds = jax.random.randint(keys[0], (EDGES,), 0, 8)
    own_rows = RIM + jax.random.randint(keys[1], (EDGES,), 0, N_DEV)
    low_rows = jax.random.randint(keys[2], (EDGES,), 0, RIM)
    high_rows = RIM + N_DEV + jax.random.randint(keys[3], (EDGES,), 0, RIM)
    first_pick = jax.random.randint(keys[4], (EDGES,), 0, N_PATCH * FAR)
    second_pick = jax.random.randint(keys[5], (EDGES,), 0, N_PATCH * FAR)
    far_rows = 2 * RIM + N_DEV + jnp.minimum(first_pick, second_pick)
    chosen = jnp.where(kinds < 4, own_rows, jnp.where(kinds == 4, low_rows, jnp.where(kinds == 5, high_rows, far_rows)))
    return chosen.astype(jnp.int32)


def plant(values, stream_key, smallest, high):
    longest = values.shape.index(max(values.shape))
    spots = []
    for shift in (0, 1):
        where = [jax.random.randint(jax.random.fold_in(stream_key, axis), (), 0, length) for axis, length in enumerate(values.shape)]
        where[longest] = (where[longest] + shift) % values.shape[longest]
        spots.append(tuple(where))
    return values.at[spots[0]].set(smallest).at[spots[1]].set(high)


def block_levels(stream_key, extent, cuts, low, high):
    def one(position, shards_of):
        steps = jax.random.uniform(jax.random.fold_in(jax.random.fold_in(stream_key, 6), position), (shards_of,), jnp.float32, low / len(cuts), high / len(cuts))
        return jnp.repeat(jnp.exp(steps), extent[position] // shards_of).reshape((-1,) + (1,) * (len(extent) - position - 1))

    level = one(*cuts[0])
    for cut in cuts[1:]:
        level = level * one(*cut)
    return level


def noise(key, extent, deviation, limit, cuts=(), kind=jnp.bfloat16):
    values = jax.random.normal(key, extent, jnp.float32) * deviation
    if len(cuts) > 0:
        values = block_levels(key, extent, cuts, -0.22, 0.18) * values
    return jnp.clip(values, min=-limit, max=limit).astype(kind)


def setup_inputs(seed: int = 0) -> dict:
    splits = jax.random.split(jax.random.key(seed), 14)
    edge_latents = noise(splits[0], (SAMPLES, EDGES, D), 1.0, 6.0, ((0, 4), (1, 64)))
    node_latents = noise(splits[1], (SAMPLES, NODES, D), 1.0, 6.0, ((0, 4), (1, 64)))
    edge_cotangent = noise(splits[2], (SAMPLES, EDGES, D), 1.0, 6.0, ((0, 4), (1, 64)))
    node_cotangent = noise(splits[3], (SAMPLES, NODES, D), 1.0, 6.0, ((0, 4), (1, 64)))
    senders = draw_senders(jax.random.fold_in(splits[13], 71), 0)
    receivers = plant(jax.random.randint(splits[5], (EDGES,), 0, N_DEV), jax.random.fold_in(splits[5], 1), 0, N_DEV - 1).astype(jnp.int32)
    send_rows = plant(jax.random.randint(splits[6], (N_PATCH * N_PATCH, FAR), 0, N_DEV), jax.random.fold_in(splits[6], 1), 0, N_DEV - 1).astype(jnp.int32)
    edge_first = noise(splits[7], (3 * D, HID), (3 * D) ** -0.5, 0.15625)
    edge_second = noise(splits[8], (HID, D), HID ** -0.5, 0.25)
    edge_gain = jnp.clip(1.0 + 0.15 * jax.random.normal(splits[9], (D,), jnp.float32), 0.25, 1.75)
    node_first = noise(splits[10], (2 * D, HID), (2 * D) ** -0.5, 0.1875)
    node_second = noise(splits[11], (HID, D), HID ** -0.5, 0.25)
    node_gain = jnp.clip(1.0 + 0.15 * jax.random.normal(splits[12], (D,), jnp.float32), 0.25, 1.75)
    return {"edge_latents": edge_latents, "node_latents": node_latents, "edge_cotangent": edge_cotangent, "node_cotangent": node_cotangent, "senders": senders, "receivers": receivers, "send_rows": send_rows, "edge_first": edge_first, "edge_second": edge_second, "edge_gain": edge_gain, "node_first": node_first, "node_second": node_second, "node_gain": node_gain}


def normalize(values):
    center = values - lax.optimization_barrier(jnp.mean(values, axis=1, keepdims=True))
    spread = lax.optimization_barrier(jnp.mean(center * center, axis=1, keepdims=True))
    scale = lax.rsqrt(spread + 1e-05)
    return (center * scale, scale)

def normalize_back(grads, normed, scale):
    first = lax.optimization_barrier(jnp.mean(grads, axis=1, keepdims=True))
    second = lax.optimization_barrier(jnp.mean(grads * normed, axis=1, keepdims=True))
    return (grads - first - normed * second) * scale

def layer_backward(edges_in, sent_latent, nodes_in, recv_ids, edge_cot, node_cot, edge_first, edge_second, edge_gain, node_first, node_second, node_gain):
    width = nodes_in.shape[1]
    recv_latent = nodes_in[recv_ids]
    edge_input = jnp.concatenate([edges_in, sent_latent, recv_latent], axis=1)
    edge_pre = jnp.dot(edge_input, edge_first, preferred_element_type=jnp.float32)
    edge_sig = jax.nn.sigmoid(edge_pre)
    edge_act = (edge_pre * edge_sig).astype(jnp.bfloat16)
    edge_raw = jnp.dot(edge_act, edge_second, preferred_element_type=jnp.float32)
    edge_hat, edge_scale = normalize(edge_raw)
    update = edge_hat * edge_gain
    inflow = jax.ops.segment_sum(update, recv_ids, num_segments=nodes_in.shape[0]).astype(jnp.bfloat16)
    node_input = jnp.concatenate([nodes_in, inflow], axis=1)
    node_pre = jnp.dot(node_input, node_first, preferred_element_type=jnp.float32)
    node_sig = jax.nn.sigmoid(node_pre)
    node_act = (node_pre * node_sig).astype(jnp.bfloat16)
    node_raw = jnp.dot(node_act, node_second, preferred_element_type=jnp.float32)
    node_hat, node_scale = normalize(node_raw)
    node_upstream = node_cot.astype(jnp.float32)
    node_gain_grad = lax.optimization_barrier(jnp.sum(node_upstream * node_hat, axis=0))
    node_raw_grad = normalize_back(node_upstream * node_gain, node_hat, node_scale).astype(jnp.bfloat16)
    node_second_grad = jnp.dot(node_act.T, node_raw_grad, preferred_element_type=jnp.float32)
    node_act_grad = jnp.dot(node_raw_grad, node_second.T, preferred_element_type=jnp.float32)
    node_pre_grad = (node_act_grad * node_sig * (1.0 + node_pre * (1.0 - node_sig))).astype(jnp.bfloat16)
    node_first_grad = jnp.dot(node_input.T, node_pre_grad, preferred_element_type=jnp.float32)
    node_input_grad = jnp.dot(node_pre_grad, node_first.T, preferred_element_type=jnp.float32)
    update_grad = edge_cot.astype(jnp.float32) + node_input_grad[:, width:][recv_ids]
    edge_gain_grad = lax.optimization_barrier(jnp.sum(update_grad * edge_hat, axis=0))
    edge_raw_grad = normalize_back(update_grad * edge_gain, edge_hat, edge_scale).astype(jnp.bfloat16)
    edge_second_grad = jnp.dot(edge_act.T, edge_raw_grad, preferred_element_type=jnp.float32)
    edge_act_grad = jnp.dot(edge_raw_grad, edge_second.T, preferred_element_type=jnp.float32)
    edge_pre_grad = (edge_act_grad * edge_sig * (1.0 + edge_pre * (1.0 - edge_sig))).astype(jnp.bfloat16)
    edge_first_grad = jnp.dot(edge_input.T, edge_pre_grad, preferred_element_type=jnp.float32)
    edge_input_grad = jnp.dot(edge_pre_grad, edge_first.T, preferred_element_type=jnp.float32)
    edge_grad = (edge_cot.astype(jnp.float32) + edge_input_grad[:, :width]).astype(jnp.bfloat16)
    sent_grad = edge_input_grad[:, width:2 * width]
    node_partial = node_upstream + node_input_grad[:, :width] + jax.ops.segment_sum(edge_input_grad[:, 2 * width:], recv_ids, num_segments=nodes_in.shape[0])
    weight_terms = (edge_first_grad, edge_second_grad, node_first_grad, node_second_grad, edge_gain_grad, node_gain_grad)
    return (edge_grad, sent_grad, node_partial, weight_terms)

def reference(edge_latents, node_latents, edge_cotangent, node_cotangent, senders, receivers, send_rows, edge_first, edge_second, edge_gain, node_first, node_second, node_gain):
    patches = N_PATCH
    device = (jnp.arange(EDGES, dtype=jnp.int32) // E_DEV).astype(jnp.int32)
    before = (device - 1) % patches
    after = (device + 1) % patches
    low_node = before * N_DEV + N_DEV - RIM + senders
    own_node = device * N_DEV + senders - RIM
    high_node = after * N_DEV + senders - RIM - N_DEV
    far_pos = jnp.clip(senders - 2 * RIM - N_DEV, 0, patches * FAR - 1)
    peer = far_pos // FAR
    far_node = peer * N_DEV + send_rows[peer * patches + device, far_pos % FAR]
    sender_node = jnp.where(senders < RIM, low_node, jnp.where(senders < RIM + N_DEV, own_node, jnp.where(senders < 2 * RIM + N_DEV, high_node, far_node))).astype(jnp.int32)
    receiver_node = (device * N_DEV + receivers).astype(jnp.int32)

    def one_sample(items):
        edges_in, nodes_in, edge_cot, node_cot = items
        edge_grad, sent_grad, node_partial, weight_terms = layer_backward(edges_in, nodes_in[sender_node], nodes_in, receiver_node, edge_cot, node_cot, edge_first, edge_second, edge_gain, node_first, node_second, node_gain)
        node_total = node_partial + jax.ops.segment_sum(sent_grad, sender_node, num_segments=NODES)
        return (edge_grad, node_total.astype(jnp.bfloat16), weight_terms)
    edge_grad, node_grad, weight_terms = lax.map(one_sample, (edge_latents, node_latents, edge_cotangent, node_cotangent))
    totals = tuple((lax.optimization_barrier(jnp.sum(term, axis=0)).astype(jnp.bfloat16) for term in weight_terms))
    return (edge_grad, node_grad, totals[0], totals[1], totals[2], totals[3], totals[4], totals[5])
```

```python
import functools

import jax
import jax.numpy as jnp
from jax import lax
from jax.experimental import pallas as pl
from jax.experimental.pallas import tpu as pltpu
from jax.sharding import PartitionSpec as P

RIM = 32
FAR = 4
MESH = pl.DeviceIdType.MESH
F32 = jnp.float32
BF16 = jnp.bfloat16
VMEM = pltpu.VMEM


def mm(a, b):
    return lax.dot_general(a, b, (((1,), (0,)), ((), ())), preferred_element_type=F32)


def mm_nt(a, b):
    return lax.dot_general(a, b, (((1,), (1,)), ((), ())), preferred_element_type=F32)


def mm_tn(a, b):
    return lax.dot_general(a, b, (((0,), (0,)), ((), ())), preferred_element_type=F32)


def one_hot_cols(col, width):
    parts = []
    lanes = lax.broadcasted_iota(jnp.int32, col.shape, 1)
    for start in range(0, width, 128):
        size = min(128, width - start)
        hit = (col == lanes + start).astype(F32).astype(BF16)
        parts.append(hit if size == 128 else hit[:, :size])
    return jnp.concatenate(parts, axis=1) if len(parts) > 1 else parts[0]


def one_hot_rows(row, height):
    ids = lax.broadcasted_iota(jnp.int32, (height, row.shape[1]), 0)
    return (ids == row).astype(F32).astype(BF16)


def normalize(values):
    center = values - jnp.mean(values, axis=1, keepdims=True)
    spread = jnp.mean(center * center, axis=1, keepdims=True)
    scale = lax.rsqrt(spread + 1e-05)
    return (center * scale, scale)


def normalize_back(grads, normed, scale):
    first = jnp.mean(grads, axis=1, keepdims=True)
    second = jnp.mean(grads * normed, axis=1, keepdims=True)
    return (grads - first - normed * second) * scale


def layer_kernel(
    lat, cot, nodes, ncot, low, high, far, senders, receivers,
    w1, w2, gain, nw1, nw2, ngain,
    edge_grad, node_partial, low_grad, high_grad, far_grad, terms, gains,
    onehot, projected, act, slope, hat, scale, raw_grad, pre_grad,
):
    edges, width = lat.shape
    count = nodes.shape[0]
    table = jnp.concatenate([low[...], nodes[...], high[...], far[...]], axis=0)
    rows = table.shape[0]
    block = 256
    projected[0:rows, :] = mm(table, w1[width : 2 * width, :]).astype(BF16)
    projected[rows : rows + count, :] = mm(nodes[...], w1[2 * width :, :]).astype(BF16)
    send_row = senders[...]
    recv_row = receivers[...]
    send_col = jnp.transpose(jnp.broadcast_to(send_row, (128, edges)))
    recv_col = jnp.transpose(jnp.broadcast_to(recv_row, (128, edges)))
    onehot[:, 0:rows] = one_hot_cols(send_col, rows)
    onehot[:, rows : rows + count] = one_hot_cols(recv_col, count)
    recv_rows = one_hot_rows(recv_row, count)
    edge_gain = gain[...]
    inflow = jnp.zeros((count, width), F32)
    for start in range(0, edges, block):
        part = slice(start, start + block)
        pre = mm(lat[part, :], w1[0:width, :]) + mm(onehot[part, :], projected[...])
        sig = jax.nn.sigmoid(pre)
        acted = (pre * sig).astype(BF16)
        act[part, :] = acted
        slope[part, :] = sig * (1.0 + pre * (1.0 - sig))
        normed, inv = normalize(mm(acted, w2[...]))
        hat[part, :] = normed
        scale[part, :] = inv
        inflow = inflow + mm(recv_rows[:, part], (normed * edge_gain).astype(BF16))
    inflow = inflow.astype(BF16)
    node_pre = mm(nodes[...], nw1[0:width, :]) + mm(inflow, nw1[width:, :])
    node_sig = jax.nn.sigmoid(node_pre)
    node_act = (node_pre * node_sig).astype(BF16)
    node_hat, node_scale = normalize(mm(node_act, nw2[...]))
    upstream = ncot[...].astype(F32)
    gains[1:2, :] = jnp.sum(upstream * node_hat, axis=0, keepdims=True)
    node_raw_grad = normalize_back(upstream * ngain[...], node_hat, node_scale).astype(BF16)
    node_act_grad = mm_nt(node_raw_grad, nw2[...])
    node_pre_grad = (node_act_grad * node_sig * (1.0 + node_pre * (1.0 - node_sig))).astype(BF16)

    def put(row, value):
        for j in range(width // 128):
            terms[j, row : row + value.shape[0], :] = value[:, 128 * j : 128 * j + 128].astype(BF16)

    put(4 * width, mm_tn(nodes[...], node_pre_grad))
    put(5 * width, mm_tn(inflow, node_pre_grad))
    put(6 * width, mm_tn(node_act, node_raw_grad))
    node_partial[...] = upstream + mm_nt(node_pre_grad, nw1[0:width, :])
    inflow_grad = mm_nt(node_pre_grad, nw1[width:, :]).astype(BF16)
    gain_grad = jnp.zeros((1, width), F32)
    for start in range(0, edges, block):
        part = slice(start, start + block)
        edge_cot = cot[part, :].astype(F32)
        normed = hat[part, :]
        update_grad = edge_cot + mm(onehot[part, rows : rows + count], inflow_grad)
        gain_grad = gain_grad + jnp.sum(update_grad * normed, axis=0, keepdims=True)
        back = normalize_back(update_grad * edge_gain, normed, scale[part, :]).astype(BF16)
        raw_grad[part, :] = back
        pre_back = (mm_nt(back, w2[...]) * slope[part, :]).astype(BF16)
        pre_grad[part, :] = pre_back
        edge_grad[part, :] = (edge_cot + mm_nt(pre_back, w1[0:width, :])).astype(BF16)
    gains[0:1, :] = gain_grad
    gains[2:8, :] = jnp.zeros((6, width), F32)
    all_pre = pre_grad[...]
    send_sum = mm(one_hot_rows(send_row, rows), all_pre).astype(BF16)
    recv_sum = mm(recv_rows, all_pre).astype(BF16)
    table_grad = mm_nt(send_sum, w1[width : 2 * width, :])
    low_grad[...] = table_grad[0:RIM, :].astype(BF16)
    high_grad[...] = table_grad[RIM + count : 2 * RIM + count, :].astype(BF16)
    far_grad[...] = table_grad[2 * RIM + count :, :].astype(BF16)
    node_partial[...] += table_grad[RIM : RIM + count, :] + mm_nt(recv_sum, w1[2 * width :, :])
    put(3 * width, mm_tn(act[...], raw_grad[...]))
    put(0, mm_tn(lat[...], all_pre))
    put(width, mm_tn(table, send_sum))
    put(2 * width, mm_tn(nodes[...], recv_sum))


def local_layer(lat, cot, nodes, ncot, low, high, far, senders, receivers, w1, w2, gain, nw1, nw2, ngain):
    edges, width = lat.shape
    count = nodes.shape[0]
    rows = count + 2 * RIM + far.shape[0]
    total = 7 * width
    shapes = (
        jax.ShapeDtypeStruct((edges, width), BF16),
        jax.ShapeDtypeStruct((count, width), F32),
        jax.ShapeDtypeStruct((RIM, width), BF16),
        jax.ShapeDtypeStruct((RIM, width), BF16),
        jax.ShapeDtypeStruct((far.shape[0], width), BF16),
        jax.ShapeDtypeStruct((width // 128, total, 128), BF16),
        jax.ShapeDtypeStruct((8, width), F32),
    )
    whole = pl.BlockSpec(memory_space=VMEM)
    return pl.pallas_call(
        layer_kernel,
        out_shape=shapes,
        in_specs=[whole] * 15,
        out_specs=(whole,) * 7,
        scratch_shapes=[
            VMEM((edges, rows + count), BF16),
            VMEM((rows + count, width), BF16),
            VMEM((edges, width), BF16),
            VMEM((edges, width), F32),
            VMEM((edges, width), F32),
            VMEM((edges, 1), F32),
            VMEM((edges, width), BF16),
            VMEM((edges, width), BF16),
        ],
        compiler_params=pltpu.CompilerParams(vmem_limit_bytes=48 * 1024 * 1024),
        cost_estimate=pl.CostEstimate(flops=8 * 10**9, bytes_accessed=20 * 10**6, transcendentals=10**6),
        name="local_layer",
    )(
        lat, cot, nodes, ncot, low, high, far, senders.reshape(1, edges), receivers.reshape(1, edges),
        w1, w2, gain.reshape(1, width), nw1, nw2, ngain.reshape(1, width),
    )


def with_halo_parts(cells, axis, width):
    count = lax.axis_size(axis)
    low = lax.ppermute(cells[cells.shape[0] - width :], axis, [(i, (i + 1) % count) for i in range(count)])
    high = lax.ppermute(cells[:width], axis, [((i + 1) % count, i) for i in range(count)])
    return low, high


def from_behind(array, axis, by):
    size = lax.axis_size(axis)
    return lax.ppermute(array, axis, [(i, (i + by) % size) for i in range(size)])


def on_device(
    edge_latents, node_latents, edge_cotangent, node_cotangent, senders, receivers, send_rows,
    edge_first, edge_second, edge_gain, node_first, node_second, node_gain,
):
    patches = lax.axis_size("patch")
    own = node_latents[0]
    count, width = own.shape
    outgoing = own[send_rows]
    far = lax.all_to_all(outgoing, "patch", split_axis=0, concat_axis=0, tiled=True).reshape(patches * FAR, width)
    low, high = with_halo_parts(own, "patch", RIM)
    edge_grad, node_partial, low_grad, high_grad, far_grad, terms, gains = local_layer(
        edge_latents[0], edge_cotangent[0], own, node_cotangent[0], low, high, far, senders, receivers,
        edge_first, edge_second, edge_gain, node_first, node_second, node_gain,
    )
    from_next = from_behind(low_grad, "patch", -1).astype(F32)
    from_prev = from_behind(high_grad, "patch", 1).astype(F32)
    returned = lax.all_to_all(
        far_grad.reshape(patches, FAR, width), "patch", split_axis=0, concat_axis=0, tiled=True
    ).astype(F32)
    node_total = node_partial + jnp.pad(from_prev, ((0, count - RIM), (0, 0)))
    node_total = node_total + jnp.pad(from_next, ((count - RIM, 0), (0, 0)))
    node_total = node_total + jax.ops.segment_sum(
        returned.reshape(patches * FAR, width), send_rows.reshape(-1), num_segments=count
    )
    summed, gains = lax.psum((terms.astype(F32), gains), ("patch", "sample"))
    summed = summed.astype(BF16)
    flat = jnp.concatenate([summed[j] for j in range(4)], axis=1)
    return (
        edge_grad[None],
        node_total.astype(BF16)[None],
        flat[: 3 * width],
        flat[3 * width : 4 * width],
        flat[4 * width : 6 * width],
        flat[6 * width :],
        gains[0].astype(BF16),
        gains[1].astype(BF16),
    )


def solution(mesh):
    return jax.shard_map(
        on_device,
        mesh=mesh,
        in_specs=(
            P("sample", "patch", None), P("sample", "patch", None), P("sample", "patch", None),
            P("sample", "patch", None), P("patch"), P("patch"), P("patch", None),
            P(), P(), P(), P(), P(), P(),
        ),
        out_specs=(P("sample", "patch", None), P("sample", "patch", None), P(), P(), P(), P(), P(), P()),
        check_vma=False,
    )
```

```python
import functools

import jax
import jax.numpy as jnp
from jax import lax
from jax.experimental import pallas as pl
from jax.experimental.pallas import tpu as pltpu
from jax.sharding import PartitionSpec as P

RIM = 32
FAR = 4
MESH = pl.DeviceIdType.MESH
F32 = jnp.float32
BF16 = jnp.bfloat16
VMEM = pltpu.VMEM


def mm(a, b):
    return lax.dot_general(a, b, (((1,), (0,)), ((), ())), preferred_element_type=F32)


def mm_nt(a, b):
    return lax.dot_general(a, b, (((1,), (1,)), ((), ())), preferred_element_type=F32)


def mm_tn(a, b):
    return lax.dot_general(a, b, (((0,), (0,)), ((), ())), preferred_element_type=F32)


def one_hot_cols(col, width):
    parts = []
    lanes = lax.broadcasted_iota(jnp.int32, col.shape, 1)
    for start in range(0, width, 128):
        size = min(128, width - start)
        hit = (col == lanes + start).astype(F32).astype(BF16)
        parts.append(hit if size == 128 else hit[:, :size])
    return jnp.concatenate(parts, axis=1) if len(parts) > 1 else parts[0]


def one_hot_rows(row, height):
    ids = lax.broadcasted_iota(jnp.int32, (height, row.shape[1]), 0)
    return (ids == row).astype(F32).astype(BF16)


def spread_far(c, rows, by_patch):
    at = lax.broadcasted_iota(jnp.int32, (4 * rows, rows), 0)
    col = lax.broadcasted_iota(jnp.int32, (4 * rows, rows), 1)
    patch, r = at // 16, at % 4
    target = patch * FAR + r if by_patch else r * (rows // FAR) + patch
    return ((col == target) & ((at // 4) % 4 == c)).astype(F32).astype(BF16)


def gather_far(c, rows, by_patch):
    at = lax.broadcasted_iota(jnp.int32, (rows, 4 * rows), 1)
    row = lax.broadcasted_iota(jnp.int32, (rows, 4 * rows), 0)
    patch, r = at // 16, at % 4
    target = patch * FAR + r if by_patch else r * (rows // FAR) + patch
    return ((row == target) & ((at // 4) % 4 == c)).astype(F32).astype(BF16)


def send_one_hot(send_rows, count):
    return jnp.concatenate([one_hot_rows(send_rows[r : r + 1, :], count) for r in range(FAR)], axis=1)


def normalize(values):
    center = values - jnp.mean(values, axis=1, keepdims=True)
    spread = jnp.mean(center * center, axis=1, keepdims=True)
    scale = lax.rsqrt(spread + 1e-05)
    return (center * scale, scale)


def normalize_back(grads, normed, scale):
    first = jnp.mean(grads, axis=1, keepdims=True)
    second = jnp.mean(grads * normed, axis=1, keepdims=True)
    return (grads - first - normed * second) * scale


def layer_kernel(
    lat, cot, nodes, ncot, low, high, far, senders, receivers,
    w1, w2, gain, nw1, nw2, ngain,
    edge_grad, node_partial, low_grad, high_grad, far_grad, terms, gains,
    onehot, projected, act, slope, hat, scale, raw_grad, pre_grad,
):
    edges, width = lat.shape
    count = nodes.shape[0]
    table = jnp.concatenate([low[...], nodes[...], high[...], far[...]], axis=0)
    rows = table.shape[0]
    block = 256
    projected[0:rows, :] = mm(table, w1[width : 2 * width, :]).astype(BF16)
    projected[rows : rows + count, :] = mm(nodes[...], w1[2 * width :, :]).astype(BF16)
    send_row = senders[...]
    recv_row = receivers[...]
    send_col = jnp.transpose(jnp.broadcast_to(send_row, (128, edges)))
    recv_col = jnp.transpose(jnp.broadcast_to(recv_row, (128, edges)))
    onehot[:, 0:rows] = one_hot_cols(send_col, rows)
    onehot[:, rows : rows + count] = one_hot_cols(recv_col, count)
    recv_rows = one_hot_rows(recv_row, count)
    edge_gain = gain[...]
    inflow = jnp.zeros((count, width), F32)
    for start in range(0, edges, block):
        part = slice(start, start + block)
        pre = mm(lat[part, :], w1[0:width, :]) + mm(onehot[part, :], projected[...])
        sig = jax.nn.sigmoid(pre)
        acted = (pre * sig).astype(BF16)
        act[part, :] = acted
        slope[part, :] = sig * (1.0 + pre * (1.0 - sig))
        normed, inv = normalize(mm(acted, w2[...]))
        hat[part, :] = normed
        scale[part, :] = inv
        inflow = inflow + mm(recv_rows[:, part], (normed * edge_gain).astype(BF16))
    inflow = inflow.astype(BF16)
    node_pre = mm(nodes[...], nw1[0:width, :]) + mm(inflow, nw1[width:, :])
    node_sig = jax.nn.sigmoid(node_pre)
    node_act = (node_pre * node_sig).astype(BF16)
    node_hat, node_scale = normalize(mm(node_act, nw2[...]))
    upstream = ncot[...].astype(F32)
    node_gain_grad = jnp.sum(upstream * node_hat, axis=0, keepdims=True)
    node_raw_grad = normalize_back(upstream * ngain[...], node_hat, node_scale).astype(BF16)
    node_act_grad = mm_nt(node_raw_grad, nw2[...])
    node_pre_grad = (node_act_grad * node_sig * (1.0 + node_pre * (1.0 - node_sig))).astype(BF16)

    def put(row, value):
        for j in range(width // 128):
            terms[j, row : row + value.shape[0], :] = value[:, 128 * j : 128 * j + 128].astype(BF16)

    put(4 * width, mm_tn(nodes[...], node_pre_grad))
    put(5 * width, mm_tn(inflow, node_pre_grad))
    put(6 * width, mm_tn(node_act, node_raw_grad))
    node_partial[...] = upstream + mm_nt(node_pre_grad, nw1[0:width, :])
    inflow_grad = mm_nt(node_pre_grad, nw1[width:, :]).astype(BF16)
    gain_grad = jnp.zeros((1, width), F32)
    for start in range(0, edges, block):
        part = slice(start, start + block)
        edge_cot = cot[part, :].astype(F32)
        normed = hat[part, :]
        update_grad = edge_cot + mm(onehot[part, rows : rows + count], inflow_grad)
        gain_grad = gain_grad + jnp.sum(update_grad * normed, axis=0, keepdims=True)
        back = normalize_back(update_grad * edge_gain, normed, scale[part, :]).astype(BF16)
        raw_grad[part, :] = back
        pre_back = (mm_nt(back, w2[...]) * slope[part, :]).astype(BF16)
        pre_grad[part, :] = pre_back
        edge_grad[part, :] = (edge_cot + mm_nt(pre_back, w1[0:width, :])).astype(BF16)
    for j in range(width // 128):
        gains[j : j + 1, :] = gain_grad[:, 128 * j : 128 * j + 128]
        gains[4 + j : 5 + j, :] = node_gain_grad[:, 128 * j : 128 * j + 128]
    all_pre = pre_grad[...]
    send_sum = mm(one_hot_rows(send_row, rows), all_pre).astype(BF16)
    recv_sum = mm(recv_rows, all_pre).astype(BF16)
    table_grad = mm_nt(send_sum, w1[width : 2 * width, :])
    low_grad[...] = table_grad[0:RIM, :].astype(BF16)
    high_grad[...] = table_grad[RIM + count : 2 * RIM + count, :].astype(BF16)
    far_rows = table_grad[2 * RIM + count :, :].astype(BF16)
    packed = jnp.zeros((4 * far_rows.shape[0], 128), F32)
    for c in range(width // 128):
        packed = packed + mm(spread_far(c, far_rows.shape[0], True), far_rows[:, 128 * c : 128 * c + 128])
    far_grad[...] = packed.astype(BF16)
    node_partial[...] += table_grad[RIM : RIM + count, :] + mm_nt(recv_sum, w1[2 * width :, :])
    put(3 * width, mm_tn(act[...], raw_grad[...]))
    put(0, mm_tn(lat[...], all_pre))
    put(width, mm_tn(table, send_sum))
    put(2 * width, mm_tn(nodes[...], recv_sum))


def local_layer(lat, cot, nodes, ncot, low, high, far, senders, receivers, w1, w2, gain, nw1, nw2, ngain):
    edges, width = lat.shape
    count = nodes.shape[0]
    rows = count + 2 * RIM + far.shape[0]
    total = 7 * width
    shapes = (
        jax.ShapeDtypeStruct((edges, width), BF16),
        jax.ShapeDtypeStruct((count, width), F32),
        jax.ShapeDtypeStruct((RIM, width), BF16),
        jax.ShapeDtypeStruct((RIM, width), BF16),
        jax.ShapeDtypeStruct((4 * far.shape[0], 128), BF16),
        jax.ShapeDtypeStruct((width // 128, total, 128), BF16),
        jax.ShapeDtypeStruct((8, 128), F32),
    )
    whole = pl.BlockSpec(memory_space=VMEM)
    return pl.pallas_call(
        layer_kernel,
        out_shape=shapes,
        in_specs=[whole] * 15,
        out_specs=(whole,) * 7,
        scratch_shapes=[
            VMEM((edges, rows + count), BF16),
            VMEM((rows + count, width), BF16),
            VMEM((edges, width), BF16),
            VMEM((edges, width), F32),
            VMEM((edges, width), F32),
            VMEM((edges, 1), F32),
            VMEM((edges, width), BF16),
            VMEM((edges, width), BF16),
        ],
        compiler_params=pltpu.CompilerParams(vmem_limit_bytes=48 * 1024 * 1024),
        cost_estimate=pl.CostEstimate(flops=8 * 10**9, bytes_accessed=20 * 10**6, transcendentals=10**6),
        name="local_layer",
    )(
        lat, cot, nodes, ncot, low, high, far, senders.reshape(1, edges), receivers.reshape(1, edges),
        w1, w2, gain.reshape(1, width), nw1, nw2, ngain.reshape(1, width),
    )


def place():
    here = lax.axis_index("patch")
    return here, lax.axis_index("sample"), lax.div(here, 16), lax.rem(lax.div(here, 2), 8), lax.rem(here, 2)


def ring(here, count, step):
    return lax.rem(here + (step + count) % count, count)


def signal(patch, sample):
    pl.semaphore_signal(
        pltpu.get_barrier_semaphore(), inc=1, device_id={"patch": patch, "sample": sample}, device_id_type=MESH
    )


def send(src, dst, send_sem, recv_sem, patch, sample):
    copy = pltpu.make_async_remote_copy(
        src_ref=src, dst_ref=dst, send_sem=send_sem, recv_sem=recv_sem,
        device_id={"patch": patch, "sample": sample}, device_id_type=MESH,
    )
    copy.start()
    return copy


def await_bytes(ref, sem):
    pltpu.make_async_copy(ref, ref, sem).wait()


def rows_at(start, size, align=16):
    return pl.ds(pl.multiple_of(start, align), size)


def exchange_kernel(nodes, send_rows, low, high, far, out, incoming, far_send, far_recv, rim_send, rim_recv):
    here, sample, _, _, _ = place()
    patches = send_rows.shape[1]
    count, width = nodes.shape
    behind, ahead = ring(here, patches, -1), ring(here, patches, 1)

    def greet(k, carry):
        signal(lax.rem(here + k, patches), sample)
        return carry

    lax.fori_loop(1, patches, greet, 0)
    chosen = mm_tn(send_one_hot(send_rows[...], count), nodes[...]).astype(BF16)
    packed = jnp.zeros(out.shape, F32)
    for c in range(width // 128):
        packed = packed + mm(spread_far(c, FAR * patches, False), chosen[:, 128 * c : 128 * c + 128])
    out[...] = packed.astype(BF16)
    pl.semaphore_wait(pltpu.get_barrier_semaphore(), patches - 1)
    rims = (
        send(nodes.at[count - RIM : count], low, rim_send.at[0], rim_recv.at[0], ahead, sample),
        send(nodes.at[0:RIM], high, rim_send.at[1], rim_recv.at[1], behind, sample),
    )

    def push(k, carry):
        to = lax.rem(here + k, patches)
        send(out.at[rows_at(to * 16, 16)], incoming.at[rows_at(here * 16, 16)], far_send, far_recv, to, sample)
        return carry

    lax.fori_loop(1, patches, push, 0)
    mine = rows_at(here * 16, 16)
    incoming[mine, :] = out[mine, :]
    await_bytes(incoming.at[0 : 16 * (patches - 1)], far_recv)
    for c in range(width // 128):
        far[:, 128 * c : 128 * c + 128] = mm(gather_far(c, FAR * patches, True), incoming[...]).astype(BF16)
    await_bytes(out.at[0 : 16 * (patches - 1)], far_send)
    for copy in rims:
        copy.wait()


def exchange(nodes, send_rows):
    count, width = nodes.shape
    patches = send_rows.shape[1]
    whole = pl.BlockSpec(memory_space=VMEM)
    return pl.pallas_call(
        exchange_kernel,
        out_shape=(
            jax.ShapeDtypeStruct((RIM, width), BF16),
            jax.ShapeDtypeStruct((RIM, width), BF16),
            jax.ShapeDtypeStruct((FAR * patches, width), BF16),
        ),
        in_specs=[whole] * 2,
        out_specs=(whole,) * 3,
        scratch_shapes=[
            VMEM((16 * patches, 128), BF16),
            VMEM((16 * patches, 128), BF16),
            pltpu.SemaphoreType.DMA,
            pltpu.SemaphoreType.DMA,
            pltpu.SemaphoreType.DMA((2,)),
            pltpu.SemaphoreType.DMA((2,)),
        ],
        compiler_params=pltpu.CompilerParams(
            collective_id=0, has_side_effects=True, vmem_limit_bytes=16 * 1024 * 1024
        ),
        name="exchange",
    )(nodes, send_rows)


def reduce_kernel(
    terms, gains, far_grad, low_grad, high_grad, node_partial, send_rows,
    total, gain_total, node_grad,
    core_in, summed, first_in, second_in, second, z_out, z_in, z_done, returned, from_prev, from_next, gain_in,
    core_sems, first_sems, second_sems, z_sems, back_sems, rim_sems, gather2_sems, gather1_sems, last_sems, gain_sems,
):
    here, x, y, z, core = place()
    patches = send_rows.shape[1]
    half = terms.shape[1] // 2
    large, small = half // 4, half // 16
    sibling = here + 1 - 2 * core
    xs = [(x, here)] + [(ring(x, 4, s), here) for s in (1, 2, 3)]
    ys = [(x, here)] + [(x, ring(y, 4, s) * 16 + z * 2 + core) for s in (1, 2, 3)]
    axes = ((x, xs), (y, ys))
    behind, ahead = ring(here, patches, -1), ring(here, patches, 1)

    def greet(k, carry):
        signal(lax.rem(here + k, patches), x)
        return carry

    for s in (1, 2, 3):
        signal(here, ring(x, 4, s))
    lax.fori_loop(1, patches, greet, 0)
    pl.semaphore_wait(pltpu.get_barrier_semaphore(), patches + 2)

    pending = []

    def post(src, dst, sems, index, device):
        copy = send(src, dst, sems.at[(0,) + index], sems.at[(1,) + index], device[1], device[0])
        pending.append(copy)
        return copy

    def pair(h):
        return slice(2 * h, 2 * h + 2)

    order = (2, 1, 3, 0)
    cores = {}
    for k, s in enumerate(order):
        for h in (0, 1):
            at = ring(axes[h][0], 4, s) * large
            cores[h, s] = post(
                terms.at[pair(h), rows_at((1 - core) * half + at, large)],
                core_in.at[pair(h), rows_at(at, large)], core_sems, (h, k), (x, sibling),
            )
    gain_copy = post(gains, gain_in.at[0], gain_sems, (0,), (x, sibling))
    rims = (
        post(high_grad, from_prev, rim_sems, (0,), (x, ahead)),
        post(low_grad, from_next, rim_sems, (1,), (x, behind)),
    )

    def push(k, carry):
        to = lax.rem(here + k, patches)
        send(
            far_grad.at[rows_at(to * 16, 16)], returned.at[rows_at(here * 16, 16)],
            back_sems.at[0], back_sems.at[1], to, x,
        )
        return carry

    def scatter(rows, size, device, pos, ready, take, source, landing, sems, h):
        copies = {}
        a, b = 2 * h, 2 * h + 1

        def chunk(s):
            return rows_at(rows(ring(pos, 4, s)), size)

        def go(index, j, s, to):
            copies[index] = post(source.at[j, chunk(s)], landing.at[h, index], sems, (h, index), device[to])

        ready(h, 2)
        go(0, a, 2, 1)
        go(1, b, 2, 3)
        ready(h, 1)
        go(2, b, 1, 1)
        ready(h, 3)
        go(3, a, 3, 3)
        return copies, chunk, go

    def relay(state, h, source, landing):
        copies, chunk, go = state
        a, b = 2 * h, 2 * h + 1
        copies[0].wait_recv()
        source[a, chunk(1)] = (source[a, chunk(1)].astype(F32) + landing[h, 0].astype(F32)).astype(BF16)
        go(4, a, 1, 1)
        copies[1].wait_recv()
        source[b, chunk(3)] = (source[b, chunk(3)].astype(F32) + landing[h, 1].astype(F32)).astype(BF16)
        go(5, b, 3, 3)

    def finish(state, h, source, landing):
        copies, chunk, _ = state
        a, b = 2 * h, 2 * h + 1
        copies[3].wait_recv()
        copies[4].wait_recv()
        first = source[a, chunk(0)].astype(F32) + landing[h, 3].astype(F32) + landing[h, 4].astype(F32)
        copies[2].wait_recv()
        copies[5].wait_recv()
        other = source[b, chunk(0)].astype(F32) + landing[h, 2].astype(F32) + landing[h, 5].astype(F32)
        return first, other

    def core_ready(h, s):
        cores[h, s].wait_recv()
        at = ring(axes[h][0], 4, s) * large
        for j in (2 * h, 2 * h + 1):
            mine = terms[j, rows_at(core * half + at, large)].astype(F32)
            summed[j, rows_at(at, large)] = (mine + core_in[j, rows_at(at, large)].astype(F32)).astype(BF16)

    states = [
        scatter(lambda q: q * large, large, axes[h][1], axes[h][0], core_ready, None, summed, first_in, first_sems, h)
        for h in (0, 1)
    ]
    lax.fori_loop(1, patches, push, 0)
    for h in (0, 1):
        core_ready(h, 0)
    gain_copy.wait_recv()
    gain_sum = jnp.where(core == 0, gains[...] + gain_in[0], gain_in[0] + gains[...])

    def share_gain(value, base, count, pos, devices, index):
        gain_in[base + pos] = value
        for s in range(1, count):
            send(
                gain_in.at[base + pos], gain_in.at[base + pos], gain_sems.at[0, index], gain_sems.at[1, index],
                devices[s][1], devices[s][0],
            )

    def gain_done(base, count, index):
        await_bytes(gain_in.at[base : base + count - 1], gain_sems.at[1, index])
        await_bytes(gain_in.at[base : base + count - 1], gain_sems.at[0, index])
        result = gain_in[base]
        for s in range(1, count):
            result = result + gain_in[base + s]
        return result

    share_gain(gain_sum, 1, 4, x, xs, 1)
    for h in (0, 1):
        relay(states[h], h, summed, first_in)
    for h in (0, 1):
        first, other = finish(states[h], h, summed, first_in)
        second[2 * h] = first.astype(BF16)
        second[2 * h + 1] = other.astype(BF16)
    swapped = (axes[1], axes[0])
    states = [
        scatter(
            lambda q: q * small, small, swapped[h][1], swapped[h][0], lambda h, s: None, None,
            second, second_in, second_sems, h,
        )
        for h in (0, 1)
    ]
    share_gain(gain_done(1, 4, 1), 5, 4, y, ys, 2)
    for h in (0, 1):
        relay(states[h], h, second, second_in)
    piece = small // 2
    z_out[...] = jnp.zeros(z_out.shape, BF16)
    for h in (0, 1):
        for j, value in enumerate(finish(states[h], h, second, second_in)):
            for k in (0, 1):
                z_out[(2 * h + j) * 2 + k, 0:piece, :] = value[piece * k : piece * (k + 1), :].astype(BF16)
    zs = [(x, here)] + [(x, y * 16 + ring(z, 8, s) * 2 + core) for s in range(1, 8)]
    for s in range(1, 8):
        send(z_out.at[ring(z, 8, s)], z_in.at[z], z_sems.at[0, 0], z_sems.at[1, 0], zs[s][1], zs[s][0])
    z_in[z] = z_out[z]
    share_gain(gain_done(5, 4, 2), 9, 8, z, zs, 3)
    await_bytes(z_in.at[0:7], z_sems.at[1, 0])
    value = z_in[0].astype(F32)
    for s in range(1, 8):
        value = value + z_in[s].astype(F32)
    z_done[z] = value.astype(BF16)
    for s in range(1, 8):
        send(z_done.at[z], z_done.at[z], z_sems.at[0, 1], z_sems.at[1, 1], zs[s][1], zs[s][0])
    gain_total[...] = gain_done(9, 8, 3)
    await_bytes(z_done.at[0:7], z_sems.at[1, 1])
    bases = [core * half + axes[h][0] * large for h in (0, 1)]
    for h in (0, 1):
        at = bases[h] + swapped[h][0] * small
        for j in (2 * h, 2 * h + 1):
            both = jnp.concatenate([z_done[2 * j, 0:piece].astype(F32), z_done[2 * j + 1, 0:piece].astype(F32)], axis=0)
            total[j, rows_at(at, small)] = both.astype(BF16)

    def spread(base, size, pos, device, sems, h):
        copies = {}
        a, b = 2 * h, 2 * h + 1

        def go(index, j, s, to):
            part = total.at[j, rows_at(base + ring(pos, 4, s) * size, size)]
            copies[index] = post(part, part, sems, (h, index), device[to])

        go(0, a, 0, 1)
        go(1, b, 0, 3)
        go(2, b, 0, 1)
        go(3, a, 0, 3)
        return copies, go

    def pass_on(state, h):
        copies, go = state
        copies[0].wait_recv()
        go(4, 2 * h, 3, 1)
        copies[1].wait_recv()
        go(5, 2 * h + 1, 1, 3)

    states = [spread(bases[h], small, swapped[h][0], swapped[h][1], gather2_sems, h) for h in (0, 1)]
    for h in (0, 1):
        pass_on(states[h], h)
    for h in (0, 1):
        for index in (2, 3, 4, 5):
            states[h][0][index].wait_recv()

    def to_sibling(k, h, s):
        part = total.at[pair(h), rows_at(core * half + ring(axes[h][0], 4, s) * large, large)]
        return post(part, part, last_sems, (h, k), (x, sibling))

    states = [spread(core * half, large, axes[h][0], axes[h][1], gather1_sems, h) for h in (0, 1)]
    last = [to_sibling(0, h, 0) for h in (0, 1)]
    await_bytes(returned.at[0 : 16 * (patches - 1)], back_sems.at[1])
    mine = rows_at(here * 16, 16)
    returned[mine, :] = far_grad[mine, :]
    for copy in rims:
        copy.wait_recv()
    width = node_partial.shape[1]
    count = node_partial.shape[0]
    back = jnp.concatenate(
        [mm(gather_far(c, FAR * patches, False), returned[...]).astype(BF16) for c in range(width // 128)], axis=1
    )
    nodes = node_partial[...] + mm(send_one_hot(send_rows[...], count), back)
    node_grad[0:RIM, :] = (nodes[0:RIM] + from_prev[...].astype(F32)).astype(BF16)
    node_grad[RIM : count - RIM, :] = nodes[RIM : count - RIM].astype(BF16)
    node_grad[count - RIM : count, :] = (nodes[count - RIM :] + from_next[...].astype(F32)).astype(BF16)
    for h in (0, 1):
        pass_on(states[h], h)
    for h in (0, 1):
        states[h][0][2].wait_recv()
        last.append(to_sibling(1, h, 3))
        states[h][0][3].wait_recv()
        last.append(to_sibling(2, h, 1))
    for h in (0, 1):
        states[h][0][4].wait_recv()
        states[h][0][5].wait_recv()
        last.append(to_sibling(3, h, 2))
    await_bytes(far_grad.at[0 : 16 * (patches - 1)], back_sems.at[0])
    await_bytes(z_out.at[0:7], z_sems.at[0, 0])
    await_bytes(z_done.at[0:7], z_sems.at[0, 1])
    for copy in last:
        copy.wait_recv()
    for copy in pending:
        copy.wait_send()


def reduce_all(terms, gains, far_grad, low_grad, high_grad, node_partial, send_rows):
    columns, rows, _ = terms.shape
    count, width = node_partial.shape
    patches = send_rows.shape[1]
    half = rows // 2
    large, small = half // 4, half // 16
    whole = pl.BlockSpec(memory_space=VMEM)
    dma = pltpu.SemaphoreType.DMA
    return pl.pallas_call(
        reduce_kernel,
        out_shape=(
            jax.ShapeDtypeStruct(terms.shape, BF16),
            jax.ShapeDtypeStruct(gains.shape, F32),
            jax.ShapeDtypeStruct((count, width), BF16),
        ),
        in_specs=[whole] * 7,
        out_specs=(whole,) * 3,
        scratch_shapes=[
            VMEM((columns, half, 128), BF16),
            VMEM((columns, half, 128), BF16),
            VMEM((2, 6, large, 128), BF16),
            VMEM((2, 6, small, 128), BF16),
            VMEM((columns, large, 128), BF16),
            VMEM((8, 64, 128), BF16),
            VMEM((8, 64, 128), BF16),
            VMEM((8, 64, 128), BF16),
            VMEM((16 * patches, 128), BF16),
            VMEM((RIM, width), BF16),
            VMEM((RIM, width), BF16),
            VMEM((17, 8, 128), F32),
            dma((2, 2, 4)),
            dma((2, 2, 6)),
            dma((2, 2, 6)),
            dma((2, 2)),
            dma((2,)),
            dma((2, 2)),
            dma((2, 2, 6)),
            dma((2, 2, 6)),
            dma((2, 2, 4)),
            dma((2, 4)),
        ],
        compiler_params=pltpu.CompilerParams(
            collective_id=1, has_side_effects=True, vmem_limit_bytes=40 * 1024 * 1024
        ),
        name="reduce_all",
    )(terms, gains, far_grad, low_grad, high_grad, node_partial, send_rows)


def on_device(
    edge_latents, node_latents, edge_cotangent, node_cotangent, senders, receivers, send_rows,
    edge_first, edge_second, edge_gain, node_first, node_second, node_gain,
):
    own = node_latents[0]
    width = own.shape[1]
    to_send = send_rows.T
    low, high, far = exchange(own, to_send)
    edge_grad, node_partial, low_grad, high_grad, far_grad, terms, gains = local_layer(
        edge_latents[0], edge_cotangent[0], own, node_cotangent[0], low, high, far, senders, receivers,
        edge_first, edge_second, edge_gain, node_first, node_second, node_gain,
    )
    summed, gains, node_grad = reduce_all(terms, gains, far_grad, low_grad, high_grad, node_partial, to_send)
    flat = jnp.concatenate([summed[j] for j in range(width // 128)], axis=1)
    gains = gains.astype(BF16).reshape(2, width)
    return (
        edge_grad[None],
        node_grad[None],
        flat[: 3 * width],
        flat[3 * width : 4 * width],
        flat[4 * width : 6 * width],
        flat[6 * width :],
        gains[0],
        gains[1],
    )


def solution(mesh):
    return jax.shard_map(
        on_device,
        mesh=mesh,
        in_specs=(
            P("sample", "patch", None), P("sample", "patch", None), P("sample", "patch", None),
            P("sample", "patch", None), P("patch"), P("patch"), P("patch", None),
            P(), P(), P(), P(), P(), P(),
        ),
        out_specs=(P("sample", "patch", None), P("sample", "patch", None), P(), P(), P(), P(), P(), P()),
        check_vma=False,
    )
```

```python
import functools

import jax
import jax.numpy as jnp
from jax import lax
from jax.experimental import pallas as pl
from jax.experimental.pallas import tpu as pltpu
from jax.sharding import PartitionSpec as P

RIM = 32
FAR = 4
MESH = pl.DeviceIdType.MESH
F32 = jnp.float32
BF16 = jnp.bfloat16
VMEM = pltpu.VMEM


def mm(a, b):
    return lax.dot_general(a, b, (((1,), (0,)), ((), ())), preferred_element_type=F32)


def mm_nt(a, b):
    return lax.dot_general(a, b, (((1,), (1,)), ((), ())), preferred_element_type=F32)


def mm_tn(a, b):
    return lax.dot_general(a, b, (((0,), (0,)), ((), ())), preferred_element_type=F32)


def one_hot_cols(col, width, first=0):
    parts = []
    lanes = lax.broadcasted_iota(jnp.int32, col.shape, 1) + first
    for start in range(0, width, 128):
        size = min(128, width - start)
        hit = (col == lanes + start).astype(F32).astype(BF16)
        parts.append(hit if size == 128 else hit[:, :size])
    return jnp.concatenate(parts, axis=1) if len(parts) > 1 else parts[0]


def one_hot_rows(row, height):
    ids = lax.broadcasted_iota(jnp.int32, (height, row.shape[1]), 0)
    return (ids == row).astype(F32).astype(BF16)


def lane_block(packed, c):
    return (lax.broadcasted_iota(jnp.int32, packed.shape, 0) // FAR) % 4 == c


def spread(rows, by_patch):
    at = lax.broadcasted_iota(jnp.int32, (4 * rows, rows), 0)
    col = lax.broadcasted_iota(jnp.int32, (4 * rows, rows), 1)
    patch, r = at // 16, at % 4
    return (col == (patch * FAR + r if by_patch else r * (rows // FAR) + patch)).astype(F32).astype(BF16)


def unspread(rows, by_patch):
    at = lax.broadcasted_iota(jnp.int32, (rows, 4 * rows), 1)
    row = lax.broadcasted_iota(jnp.int32, (rows, 4 * rows), 0)
    patch, r = at // 16, at % 4
    return (row == (patch * FAR + r if by_patch else r * (rows // FAR) + patch)).astype(F32).astype(BF16)


def pack(values, by_patch):
    wide = mm(spread(values.shape[0], by_patch), values)
    packed = wide[:, 0:128]
    for c in (1, 2, 3):
        packed = jnp.where(lane_block(packed, c), wide[:, 128 * c : 128 * c + 128], packed)
    return packed.astype(BF16)


def unpack(packed, by_patch):
    values = packed.astype(F32)
    wide = jnp.concatenate([jnp.where(lane_block(values, c), values, 0.0).astype(BF16) for c in range(4)], axis=1)
    return mm(unspread(packed.shape[0] // 4, by_patch), wide).astype(BF16)


def send_one_hot(send_rows, count):
    return jnp.concatenate([one_hot_rows(send_rows[r : r + 1, :], count) for r in range(FAR)], axis=1)


def normalize(values):
    center = values - jnp.mean(values, axis=1, keepdims=True)
    spread = jnp.mean(center * center, axis=1, keepdims=True)
    scale = lax.rsqrt(spread + 1e-05)
    return (center * scale, scale)


def normalize_back(grads, normed, scale):
    first = jnp.mean(grads, axis=1, keepdims=True)
    second = jnp.mean(grads * normed, axis=1, keepdims=True)
    return (grads - first - normed * second) * scale


def place():
    here = lax.axis_index("patch")
    return here, lax.axis_index("sample"), lax.div(here, 16), lax.rem(lax.div(here, 2), 8), lax.rem(here, 2)


def ring(here, count, step):
    return lax.rem(here + (step + count) % count, count)


def signal(patch, sample):
    pl.semaphore_signal(
        pltpu.get_barrier_semaphore(), inc=1, device_id={"patch": patch, "sample": sample}, device_id_type=MESH
    )


def send(src, dst, send_sem, recv_sem, patch, sample):
    copy = pltpu.make_async_remote_copy(
        src_ref=src, dst_ref=dst, send_sem=send_sem, recv_sem=recv_sem,
        device_id={"patch": patch, "sample": sample}, device_id_type=MESH,
    )
    copy.start()
    return copy


def await_bytes(ref, sem):
    pltpu.make_async_copy(ref, ref, sem).wait()


def rows_at(start, size, align=16):
    return pl.ds(pl.multiple_of(start, align), size)


def reduction(terms, total, where, scratch, pending):
    x, y, z, core, here, xs, ys, zs = where
    core_in, summed, first_in, second, second_in, z_out, z_in, z_done, sems, z_sems = scratch
    half = terms.shape[1] // 2
    large, small = half // 4, half // 16
    piece = small // 2
    sibling = here + 1 - 2 * core
    outer = ((x, xs), (y, ys))
    inner = ((y, ys), (x, xs))
    both = (0, 1)

    def post(src, dst, index, device):
        copy = send(src, dst, sems.at[(0,) + index], sems.at[(1,) + index], device[1], device[0])
        pending.append(copy)
        return copy

    def pair(h):
        return slice(2 * h, 2 * h + 2)

    def chunk(axis, s, size):
        return ring(axis[0], 4, s) * size

    copies = {}
    for k, s in enumerate((2, 1, 3, 0)):
        for h in both:
            at = chunk(outer[h], s, large)
            copies[h, s] = post(
                terms.at[pair(h), rows_at((1 - core) * half + at, large)],
                core_in.at[pair(h), rows_at(at, large)], (0, h, s), (x, sibling),
            )
    yield

    def core_ready(h, s):
        copies[h, s].wait_recv()
        at = chunk(outer[h], s, large)
        for j in (2 * h, 2 * h + 1):
            mine = terms[j, rows_at(core * half + at, large)].astype(F32)
            summed[j, rows_at(at, large)] = (mine + core_in[j, rows_at(at, large)].astype(F32)).astype(BF16)

    first = {}
    for s in (2, 1, 3):
        for h in both:
            core_ready(h, s)
            first[h, s] = post(
                summed.at[pair(h), rows_at(chunk(outer[h], s, large), large)], first_in.at[h, s - 1],
                (1, h, s), outer[h][1][s],
            )
    for h in both:
        core_ready(h, 0)
    yield

    def collect(h, j, source, at, size, landing):
        value = source[2 * h + j, rows_at(at, size)].astype(F32)
        for s in (1, 2, 3):
            value = value + landing[h, s - 1, j].astype(F32)
        return value

    then = {}
    for h in both:
        for s in (1, 2, 3):
            first[h, s].wait_recv()
        for j in both:
            second[2 * h + j] = collect(h, j, summed, chunk(outer[h], 0, large), large, first_in).astype(BF16)
        for s in (2, 1, 3):
            then[h, s] = post(
                second.at[pair(h), rows_at(chunk(inner[h], s, small), small)], second_in.at[h, s - 1],
                (2, h, s), inner[h][1][s],
            )
    yield
    if z_out.shape[1] > piece:
        z_out[...] = jnp.zeros(z_out.shape, BF16)
    for h in both:
        for s in (1, 2, 3):
            then[h, s].wait_recv()
        for j in both:
            value = collect(h, j, second, chunk(inner[h], 0, small), small, second_in).astype(BF16)
            for k in both:
                z_out[(2 * h + j) * 2 + k, 0:piece, :] = value[piece * k : piece * (k + 1), :]
    for s in (4, 3, 5, 2, 6, 1, 7):
        send(z_out.at[ring(z, 8, s)], z_in.at[z], z_sems.at[0, 0], z_sems.at[1, 0], zs[s][1], zs[s][0])
    z_in[z] = z_out[z]
    yield
    await_bytes(z_in.at[0:7], z_sems.at[1, 0])
    value = z_in[0].astype(F32)
    for s in range(1, 8):
        value = value + z_in[s].astype(F32)
    z_done[z] = value.astype(BF16)
    for s in (4, 3, 5, 2, 6, 1, 7):
        send(z_done.at[z], z_done.at[z], z_sems.at[0, 1], z_sems.at[1, 1], zs[s][1], zs[s][0])
    yield
    await_bytes(z_done.at[0:7], z_sems.at[1, 1])
    back = {}

    def share(h, base, axis, size, stage):
        part = total.at[pair(h), rows_at(base + axis[0] * size, size)]
        for s in (2, 1, 3):
            back[stage, h, s] = post(part, part, (stage, h, s), axis[1][s])

    bases = [core * half + chunk(outer[h], 0, large) for h in both]
    for h in both:
        at = bases[h] + chunk(inner[h], 0, small)
        for j in (2 * h, 2 * h + 1):
            joined = jnp.concatenate([z_done[2 * j + k, 0:piece].astype(F32) for k in both], axis=0)
            total[j, rows_at(at, small)] = joined.astype(BF16)
        share(h, bases[h], inner[h], small, 3)
    yield
    for h in both:
        for s in (1, 2, 3):
            back[3, h, s].wait_recv()
        share(h, core * half, outer[h], large, 4)
    last = []

    def to_sibling(h, s):
        part = total.at[pair(h), rows_at(core * half + chunk(outer[h], -s, large), large)]
        last.append(post(part, part, (5, h, s), (x, sibling)))

    for h in both:
        to_sibling(h, 0)
    yield
    for s in (1, 3, 2):
        for h in both:
            back[4, h, s].wait_recv()
            to_sibling(h, s)
    yield
    for copy in last:
        copy.wait_recv()
    await_bytes(z_out.at[0:7], z_sems.at[0, 0])
    await_bytes(z_done.at[0:7], z_sems.at[0, 1])


def gain_reduction(value, result, where, slots, sems):
    x, y, z, core, here, xs, ys, zs = where
    cores = [(x, here), (x, here + 1 - 2 * core)]
    base = 0
    for index, (count, pos, devices) in enumerate(((2, core, cores), (4, x, xs), (4, y, ys), (8, z, zs))):
        slots[base + pos] = value
        for s in range(1, count):
            mine = slots.at[base + pos]
            send(mine, mine, sems.at[0, index], sems.at[1, index], devices[s][1], devices[s][0])
        yield
        await_bytes(slots.at[base : base + count - 1], sems.at[1, index])
        await_bytes(slots.at[base : base + count - 1], sems.at[0, index])
        value = slots[base]
        for s in range(1, count):
            value = value + slots[base + s]
        base += count
    result[...] = value


def advance(step):
    next(step, None)


def layer_kernel(
    nodes, send_rows, senders, receivers, gain, ngain, lat_in, cot_in, ncot_in, w1_in, w2_in, nw1_in, nw2_in,
    edge_grad, node_grad, edge_total, node_total, gain_total,
    lat, cot, ncot, w1, w2, nw1, nw2, others, packed, incoming, far_grad, returned, rim_grad, from_rims,
    onehot, projected, act, slope, hat, scale, raw_grad, pre_grad, node_partial, edge_terms, node_terms, slots, *rest,
):
    edge_scratch, node_scratch = rest[0:10], rest[10:20]
    load_sems, far_sems, rim_sems, back_sems, back_rim_sems, gain_sems = rest[20:]
    here, x, y, z, core = place()
    edges, width = lat.shape
    count = nodes.shape[0]
    patches = send_rows.shape[1]
    outside = others.shape[0]
    rows = count + outside
    block = 256
    xs = [(x, here)] + [(ring(x, 4, s), here) for s in (1, 2, 3)]
    ys = [(x, here)] + [(x, ring(y, 4, s) * 16 + z * 2 + core) for s in (1, 2, 3)]
    zs = [(x, here)] + [(x, y * 16 + ring(z, 8, s) * 2 + core) for s in range(1, 8)]
    where = (x, y, z, core, here, xs, ys, zs)
    behind, ahead = ring(here, patches, -1), ring(here, patches, 1)

    loads = [
        pltpu.make_async_copy(src, dst, load_sems.at[k])
        for k, (src, dst) in enumerate(
            ((w1_in, w1), (lat_in, lat), (w2_in, w2), (nw1_in, nw1), (nw2_in, nw2), (ncot_in, ncot), (cot_in, cot))
        )
    ]
    for copy in loads:
        copy.start()

    def greet(k, carry):
        signal(lax.rem(here + k, patches), x)
        return carry

    lax.fori_loop(1, patches, greet, 0)
    for s in (1, 2, 3):
        signal(here, ring(x, 4, s))
    spread_nodes = send_one_hot(send_rows[...], count)
    packed[...] = pack(mm_tn(spread_nodes, nodes[...]).astype(BF16), False)
    pl.semaphore_wait(pltpu.get_barrier_semaphore(), patches + 2)
    rims = (
        send(nodes.at[count - RIM : count], others.at[0:RIM], rim_sems.at[0, 0], rim_sems.at[1, 0], ahead, x),
        send(nodes.at[0:RIM], others.at[RIM : 2 * RIM], rim_sems.at[0, 1], rim_sems.at[1, 1], behind, x),
    )

    def push(src, dst, sems):
        def one(k, carry):
            to = lax.rem(here + k, patches)
            send(src.at[rows_at(to * 16, 16)], dst.at[rows_at(here * 16, 16)], sems.at[0], sems.at[1], to, x)
            return carry

        lax.fori_loop(1, patches, one, 0)

    mine = rows_at(here * 16, 16)
    all_but_mine = slice(0, 16 * (patches - 1))
    push(packed, incoming, far_sems)

    send_row, recv_row = senders[...], receivers[...]
    table_row = jnp.where(send_row < RIM, send_row + count, jnp.where(send_row < RIM + count, send_row - RIM, send_row))
    send_col = jnp.transpose(jnp.broadcast_to(table_row, (128, edges)))
    recv_col = jnp.transpose(jnp.broadcast_to(recv_row, (128, edges)))
    onehot[:, 0:count] = one_hot_cols(send_col, count)
    onehot[:, count : 2 * count] = one_hot_cols(recv_col, count)
    onehot[:, 2 * count : 2 * count + outside] = one_hot_cols(send_col, outside, count)
    recv_rows = one_hot_rows(recv_row, count)
    loads[0].wait()
    projected[0:count, :] = mm(nodes[...], w1[width : 2 * width, :]).astype(BF16)
    projected[count : 2 * count, :] = mm(nodes[...], w1[2 * width :, :]).astype(BF16)
    loads[1].wait()
    for start in range(0, edges, block):
        part = slice(start, start + block)
        slope[part, :] = mm(lat[part, :], w1[0:width, :]) + mm(onehot[part, 0 : 2 * count], projected[0 : 2 * count, :])

    for copy in rims:
        copy.wait_recv()
    incoming[mine, :] = packed[mine, :]
    await_bytes(incoming.at[all_but_mine], far_sems.at[1])
    others[2 * RIM :, :] = unpack(incoming[...], True)
    projected[2 * count : 2 * count + outside, :] = mm(others[...], w1[width : 2 * width, :]).astype(BF16)
    loads[2].wait()
    edge_gain = gain[...]
    inflow = jnp.zeros((count, width), F32)
    for start in range(0, edges, block):
        part = slice(start, start + block)
        pre = slope[part, :] + mm(onehot[part, 2 * count :], projected[2 * count :, :])
        sig = jax.nn.sigmoid(pre)
        acted = (pre * sig).astype(BF16)
        act[part, :] = acted
        slope[part, :] = sig * (1.0 + pre * (1.0 - sig))
        normed, inv = normalize(mm(acted, w2[...]))
        hat[part, :] = normed
        scale[part, :] = inv
        inflow = inflow + mm(recv_rows[:, part], (normed * edge_gain).astype(BF16))
    inflow = inflow.astype(BF16)
    for copy in loads[3:]:
        copy.wait()
    node_pre = mm(nodes[...], nw1[0:width, :]) + mm(inflow, nw1[width:, :])
    node_sig = jax.nn.sigmoid(node_pre)
    node_act = (node_pre * node_sig).astype(BF16)
    node_hat, node_scale = normalize(mm(node_act, nw2[...]))
    upstream = ncot[...].astype(F32)
    node_gain_grad = jnp.sum(upstream * node_hat, axis=0, keepdims=True)
    node_raw_grad = normalize_back(upstream * ngain[...], node_hat, node_scale).astype(BF16)
    node_act_grad = mm_nt(node_raw_grad, nw2[...])
    node_pre_grad = (node_act_grad * node_sig * (1.0 + node_pre * (1.0 - node_sig))).astype(BF16)

    def put(terms, row, value):
        for j in range(width // 128):
            terms[j, row : row + value.shape[0], :] = value[:, 128 * j : 128 * j + 128].astype(BF16)

    put(node_terms, 0, mm_tn(nodes[...], node_pre_grad))
    put(node_terms, width, mm_tn(inflow, node_pre_grad))
    put(node_terms, 2 * width, mm_tn(node_act, node_raw_grad))
    pending = []
    node_sum = reduction(node_terms, node_total, where, node_scratch, pending)
    advance(node_sum)
    node_partial[...] = upstream + mm_nt(node_pre_grad, nw1[0:width, :])
    inflow_grad = mm_nt(node_pre_grad, nw1[width:, :]).astype(BF16)
    gain_grad = jnp.zeros((1, width), F32)
    for start in range(0, edges, block):
        part = slice(start, start + block)
        edge_cot = cot[part, :].astype(F32)
        normed = hat[part, :]
        update_grad = edge_cot + mm(onehot[part, count : 2 * count], inflow_grad)
        gain_grad = gain_grad + jnp.sum(update_grad * normed, axis=0, keepdims=True)
        back = normalize_back(update_grad * edge_gain, normed, scale[part, :]).astype(BF16)
        raw_grad[part, :] = back
        pre_back = (mm_nt(back, w2[...]) * slope[part, :]).astype(BF16)
        pre_grad[part, :] = pre_back
        edge_grad[part, :] = (edge_cot + mm_nt(pre_back, w1[0:width, :])).astype(BF16)
        if start == 0:
            advance(node_sum)
    all_pre = pre_grad[...]
    put(edge_terms, 3 * width, mm_tn(act[...], raw_grad[...]))
    put(edge_terms, 0, mm_tn(lat[...], all_pre))
    send_sum = mm(one_hot_rows(table_row, rows), all_pre).astype(BF16)
    recv_sum = mm(recv_rows, all_pre).astype(BF16)
    put(edge_terms, width, mm_tn(nodes[...], send_sum[0:count]) + mm_tn(others[...], send_sum[count:]))
    put(edge_terms, 2 * width, mm_tn(nodes[...], recv_sum))
    edge_sum = reduction(edge_terms, edge_total, where, edge_scratch, pending)
    advance(edge_sum)
    advance(node_sum)
    gain_rows = [gain_grad[:, 128 * j : 128 * j + 128] for j in range(width // 128)]
    gain_rows += [node_gain_grad[:, 128 * j : 128 * j + 128] for j in range(width // 128)]
    gain_sum = gain_reduction(jnp.concatenate(gain_rows, axis=0), gain_total, where, slots, gain_sems)
    advance(gain_sum)
    other_grad = mm_nt(send_sum[count:], w1[width : 2 * width, :]).astype(BF16)
    rim_grad[...] = other_grad[0 : 2 * RIM]
    back_rims = (
        send(rim_grad.at[RIM : 2 * RIM], from_rims.at[0:RIM], back_rim_sems.at[0, 0], back_rim_sems.at[1, 0], ahead, x),
        send(rim_grad.at[0:RIM], from_rims.at[RIM : 2 * RIM], back_rim_sems.at[0, 1], back_rim_sems.at[1, 1], behind, x),
    )
    advance(edge_sum)
    far_grad[...] = pack(other_grad[2 * RIM :], True)
    push(far_grad, returned, back_sems)
    node_partial[...] += mm_nt(send_sum[0:count], w1[width : 2 * width, :]) + mm_nt(recv_sum, w1[2 * width :, :])
    advance(node_sum)
    advance(gain_sum)
    returned[mine, :] = far_grad[mine, :]
    advance(edge_sum)
    advance(node_sum)
    advance(gain_sum)
    for copy in back_rims:
        copy.wait_recv()
    await_bytes(returned.at[all_but_mine], back_sems.at[1])
    nodes_done = node_partial[...] + mm(spread_nodes, unpack(returned[...], False))
    node_grad[0:RIM, :] = (nodes_done[0:RIM] + from_rims[0:RIM].astype(F32)).astype(BF16)
    node_grad[RIM : count - RIM, :] = nodes_done[RIM : count - RIM].astype(BF16)
    node_grad[count - RIM : count, :] = (nodes_done[count - RIM :] + from_rims[RIM : 2 * RIM].astype(F32)).astype(BF16)
    advance(edge_sum)
    advance(node_sum)
    advance(gain_sum)
    for _ in range(8):
        advance(edge_sum)
        advance(node_sum)
    advance(gain_sum)
    for copy in rims + back_rims:
        copy.wait_send()
    await_bytes(packed.at[all_but_mine], far_sems.at[0])
    await_bytes(far_grad.at[all_but_mine], back_sems.at[0])
    for copy in pending:
        copy.wait_send()


def place_kernel(
    edge_total, node_total, edge_in, node_in, gains, first, second, nfirst, nsecond, edge_out, node_out, gain_out, ngain_out,
    edge_in_v, node_in_v, edge_v, rows_v, nfirst_v, nsecond_v, first_v, second_v, in_sems, out_sems,
):
    width = first.shape[1]
    starts = []
    for k, (src, dst) in enumerate(
        ((edge_total, edge_in_v), (node_total, node_in_v), (edge_in, edge_v), (node_in, rows_v))
    ):
        starts.append(pltpu.make_async_copy(src, dst, in_sems.at[k]))
        starts[-1].start()
    ends = []

    def out(src, dst):
        ends.append(pltpu.make_async_copy(src, dst, out_sems.at[len(ends)]))
        ends[-1].start()

    def relay(source, first, dst):
        rows = dst.shape[0]
        for j in range(width // 128):
            dst[:, 128 * j : 128 * j + 128] = source[j, first : first + rows, :]

    for j in range(width // 128):
        cols = slice(128 * j, 128 * j + 128)
        gain_out[cols] = gains[j, :].astype(BF16)
        ngain_out[cols] = gains[4 + j, :].astype(BF16)
    starts[0].wait()
    relay(edge_in_v, 0, first_v)
    out(first_v, first)
    relay(edge_in_v, 3 * width, second_v)
    out(second_v, second)
    starts[1].wait()
    relay(node_in_v, 0, nfirst_v)
    out(nfirst_v, nfirst)
    relay(node_in_v, 2 * width, nsecond_v)
    out(nsecond_v, nsecond)
    starts[2].wait()
    out(edge_v, edge_out)
    starts[3].wait()
    out(rows_v, node_out)
    for copy in ends:
        copy.wait()


def place_results(edge_total, node_total, edge_grad, node_grad, gains):
    width = edge_grad.shape[1]
    anywhere, whole = pl.BlockSpec(memory_space=pl.ANY), pl.BlockSpec(memory_space=VMEM)
    return pl.pallas_call(
        place_kernel,
        out_shape=tuple(
            jax.ShapeDtypeStruct(shape, BF16)
            for shape in (
                (3 * width, width), (width, width), (2 * width, width), (width, width),
                edge_grad.shape, node_grad.shape, (width,), (width,),
            )
        ),
        in_specs=[anywhere] * 4 + [whole],
        out_specs=(anywhere,) * 6 + (whole,) * 2,
        scratch_shapes=[
            VMEM(edge_total.shape, BF16),
            VMEM(node_total.shape, BF16),
            VMEM(edge_grad.shape, BF16),
            VMEM(node_grad.shape, BF16),
            VMEM((2 * width, width), BF16),
            VMEM((width, width), BF16),
            VMEM((3 * width, width), BF16),
            VMEM((width, width), BF16),
            pltpu.SemaphoreType.DMA((4,)),
            pltpu.SemaphoreType.DMA((6,)),
        ],
        compiler_params=pltpu.CompilerParams(vmem_limit_bytes=56 * 1024 * 1024),
        name="place_results",
    )(edge_total, node_total, edge_grad, node_grad, gains)


def reduction_scratch(total):
    half = total // 2
    large, small = half // 4, half // 16
    padded = -(-(small // 2) // 16) * 16
    dma = pltpu.SemaphoreType.DMA
    return [
        VMEM((4, half, 128), BF16),
        VMEM((4, half, 128), BF16),
        VMEM((2, 3, 2, large, 128), BF16),
        VMEM((4, large, 128), BF16),
        VMEM((2, 3, 2, small, 128), BF16),
        VMEM((8, padded, 128), BF16),
        VMEM((8, padded, 128), BF16),
        VMEM((8, padded, 128), BF16),
        dma((2, 6, 2, 4)),
        dma((2, 2)),
    ]


def layer(lat, cot, nodes, ncot, senders, receivers, send_rows, w1, w2, gain, nw1, nw2, ngain):
    edges, width = lat.shape
    count = nodes.shape[0]
    patches = send_rows.shape[1]
    outside = 2 * RIM + FAR * patches
    anywhere, whole = pl.BlockSpec(memory_space=pl.ANY), pl.BlockSpec(memory_space=VMEM)
    dma = pltpu.SemaphoreType.DMA
    packed = VMEM((16 * patches, 128), BF16)
    return pl.pallas_call(
        layer_kernel,
        out_shape=(
            jax.ShapeDtypeStruct((edges, width), BF16),
            jax.ShapeDtypeStruct((count, width), BF16),
            jax.ShapeDtypeStruct((4, 4 * width, 128), BF16),
            jax.ShapeDtypeStruct((4, 3 * width, 128), BF16),
            jax.ShapeDtypeStruct((8, 128), F32),
        ),
        in_specs=[whole] * 6 + [anywhere] * 7,
        out_specs=(whole,) * 5,
        scratch_shapes=[
            VMEM(lat.shape, BF16),
            VMEM(cot.shape, BF16),
            VMEM(ncot.shape, BF16),
            VMEM(w1.shape, BF16),
            VMEM(w2.shape, BF16),
            VMEM(nw1.shape, BF16),
            VMEM(nw2.shape, BF16),
            VMEM((outside, width), BF16),
            packed,
            packed,
            packed,
            packed,
            VMEM((2 * RIM, width), BF16),
            VMEM((2 * RIM, width), BF16),
            VMEM((edges, 2 * count + outside), BF16),
            VMEM((2 * count + outside, width), BF16),
            VMEM((edges, width), BF16),
            VMEM((edges, width), F32),
            VMEM((edges, width), F32),
            VMEM((edges, 1), F32),
            VMEM((edges, width), BF16),
            VMEM((edges, width), BF16),
            VMEM((count, width), F32),
            VMEM((4, 4 * width, 128), BF16),
            VMEM((4, 3 * width, 128), BF16),
            VMEM((18, 8, 128), F32),
        ]
        + reduction_scratch(4 * width)
        + reduction_scratch(3 * width)
        + [dma((7,)), dma((2,)), dma((2, 2)), dma((2,)), dma((2, 2)), dma((2, 4))],
        compiler_params=pltpu.CompilerParams(
            collective_id=0, has_side_effects=True, vmem_limit_bytes=56 * 1024 * 1024
        ),
        name="layer",
    )(
        nodes, send_rows, senders.reshape(1, edges), receivers.reshape(1, edges),
        gain.reshape(1, width), ngain.reshape(1, width), lat, cot, ncot, w1, w2, nw1, nw2,
    )


def on_device(
    edge_latents, node_latents, edge_cotangent, node_cotangent, senders, receivers, send_rows,
    edge_first, edge_second, edge_gain, node_first, node_second, node_gain,
):
    width = edge_first.shape[1]
    edge_grad, node_grad, edge_total, node_total, gains = layer(
        edge_latents[0], edge_cotangent[0], node_latents[0], node_cotangent[0], senders, receivers, send_rows.T,
        edge_first, edge_second, edge_gain, node_first, node_second, node_gain,
    )
    first, second, nfirst, nsecond, edge_grad, node_grad, gain_grad, ngain_grad = place_results(
        edge_total, node_total, edge_grad, node_grad, gains
    )
    return (
        edge_grad[None], node_grad[None], first, second, nfirst, nsecond,
        gain_grad, ngain_grad,
    )


def solution(mesh):
    return jax.shard_map(
        on_device,
        mesh=mesh,
        in_specs=(
            P("sample", "patch", None), P("sample", "patch", None), P("sample", "patch", None),
            P("sample", "patch", None), P("patch"), P("patch"), P("patch", None),
            P(), P(), P(), P(), P(), P(),
        ),
        out_specs=(P("sample", "patch", None), P("sample", "patch", None), P(), P(), P(), P(), P(), P()),
        check_vma=False,
    )
```

```python
import functools

import jax
import jax.numpy as jnp
from jax import lax
from jax.experimental import pallas as pl
from jax.experimental.pallas import tpu as pltpu
from jax.sharding import PartitionSpec as P

RIM = 32
FAR = 4
MESH = pl.DeviceIdType.MESH
F32 = jnp.float32
BF16 = jnp.bfloat16
VMEM = pltpu.VMEM


def mm(a, b):
    return lax.dot_general(a, b, (((1,), (0,)), ((), ())), preferred_element_type=F32)


def mm_nt(a, b):
    return lax.dot_general(a, b, (((1,), (1,)), ((), ())), preferred_element_type=F32)


def mm_tn(a, b):
    return lax.dot_general(a, b, (((0,), (0,)), ((), ())), preferred_element_type=F32)


def one_hot_cols(col, width, first=0):
    parts = []
    lanes = lax.broadcasted_iota(jnp.int32, col.shape, 1) + first
    for start in range(0, width, 128):
        size = min(128, width - start)
        hit = (col == lanes + start).astype(F32).astype(BF16)
        parts.append(hit if size == 128 else hit[:, :size])
    return jnp.concatenate(parts, axis=1) if len(parts) > 1 else parts[0]


def one_hot_rows(row, height):
    ids = lax.broadcasted_iota(jnp.int32, (height, row.shape[1]), 0)
    return (ids == row).astype(F32).astype(BF16)


def lane_block(packed, c):
    return (lax.broadcasted_iota(jnp.int32, packed.shape, 0) // FAR) % 4 == c


def spread(rows, by_patch):
    at = lax.broadcasted_iota(jnp.int32, (4 * rows, rows), 0)
    col = lax.broadcasted_iota(jnp.int32, (4 * rows, rows), 1)
    patch, r = at // 16, at % 4
    return (col == (patch * FAR + r if by_patch else r * (rows // FAR) + patch)).astype(F32).astype(BF16)


def unspread(rows, by_patch):
    at = lax.broadcasted_iota(jnp.int32, (rows, 4 * rows), 1)
    row = lax.broadcasted_iota(jnp.int32, (rows, 4 * rows), 0)
    patch, r = at // 16, at % 4
    return (row == (patch * FAR + r if by_patch else r * (rows // FAR) + patch)).astype(F32).astype(BF16)


def pack(values, by_patch):
    wide = mm(spread(values.shape[0], by_patch), values)
    packed = wide[:, 0:128]
    for c in (1, 2, 3):
        packed = jnp.where(lane_block(packed, c), wide[:, 128 * c : 128 * c + 128], packed)
    return packed.astype(BF16)


def unpack(packed, by_patch):
    values = packed.astype(F32)
    wide = jnp.concatenate([jnp.where(lane_block(values, c), values, 0.0).astype(BF16) for c in range(4)], axis=1)
    return mm(unspread(packed.shape[0] // 4, by_patch), wide).astype(BF16)


def send_one_hot(send_rows, count):
    return jnp.concatenate([one_hot_rows(send_rows[r : r + 1, :], count) for r in range(FAR)], axis=1)


def normalize(values):
    center = values - jnp.mean(values, axis=1, keepdims=True)
    spread = jnp.mean(center * center, axis=1, keepdims=True)
    scale = lax.rsqrt(spread + 1e-05)
    return (center * scale, scale)


def normalize_back(grads, normed, scale):
    first = jnp.mean(grads, axis=1, keepdims=True)
    second = jnp.mean(grads * normed, axis=1, keepdims=True)
    return (grads - first - normed * second) * scale


def place():
    here = lax.axis_index("patch")
    return here, lax.axis_index("sample"), lax.div(here, 16), lax.rem(lax.div(here, 2), 8), lax.rem(here, 2)


def ring(here, count, step):
    return lax.rem(here + (step + count) % count, count)


def signal(patch, sample):
    pl.semaphore_signal(
        pltpu.get_barrier_semaphore(), inc=1, device_id={"patch": patch, "sample": sample}, device_id_type=MESH
    )


def send(src, dst, send_sem, recv_sem, patch, sample):
    copy = pltpu.make_async_remote_copy(
        src_ref=src, dst_ref=dst, send_sem=send_sem, recv_sem=recv_sem,
        device_id={"patch": patch, "sample": sample}, device_id_type=MESH,
    )
    copy.start()
    return copy


def await_bytes(ref, sem):
    pltpu.make_async_copy(ref, ref, sem).wait()


def rows_at(start, size, align=16):
    return pl.ds(pl.multiple_of(start, align), size)


def reduction(terms, total, where, scratch, pending):
    x, y, z, core, here, xs, ys, zs = where
    core_in, summed, first_in, second, second_in, z_out, z_in, z_done, sems, z_sems = scratch
    half = terms.shape[1] // 2
    large, small = half // 4, half // 16
    piece = small // 2
    sibling = here + 1 - 2 * core
    outer = ((x, xs), (y, ys))
    inner = ((y, ys), (x, xs))
    both = (0, 1)

    def post(src, dst, index, device):
        copy = send(src, dst, sems.at[(0,) + index], sems.at[(1,) + index], device[1], device[0])
        pending.append(copy)
        return copy

    def pair(h):
        return slice(2 * h, 2 * h + 2)

    def chunk(axis, s, size):
        return ring(axis[0], 4, s) * size

    copies = {}
    for k, s in enumerate((2, 1, 3, 0)):
        for h in both:
            at = chunk(outer[h], s, large)
            copies[h, s] = post(
                terms.at[pair(h), rows_at((1 - core) * half + at, large)],
                core_in.at[pair(h), rows_at(at, large)], (0, h, s), (x, sibling),
            )
    yield

    def core_ready(h, s):
        copies[h, s].wait_recv()
        at = chunk(outer[h], s, large)
        for j in (2 * h, 2 * h + 1):
            mine = terms[j, rows_at(core * half + at, large)].astype(F32)
            summed[j, rows_at(at, large)] = (mine + core_in[j, rows_at(at, large)].astype(F32)).astype(BF16)

    first = {}
    for s in (2, 1, 3):
        for h in both:
            core_ready(h, s)
            first[h, s] = post(
                summed.at[pair(h), rows_at(chunk(outer[h], s, large), large)], first_in.at[h, s - 1],
                (1, h, s), outer[h][1][s],
            )
    for h in both:
        core_ready(h, 0)
    yield

    def collect(h, j, source, at, size, landing):
        value = source[2 * h + j, rows_at(at, size)].astype(F32)
        for s in (1, 2, 3):
            value = value + landing[h, s - 1, j].astype(F32)
        return value

    then = {}
    for h in both:
        for s in (1, 2, 3):
            first[h, s].wait_recv()
        for j in both:
            second[2 * h + j] = collect(h, j, summed, chunk(outer[h], 0, large), large, first_in).astype(BF16)
        for s in (2, 1, 3):
            then[h, s] = post(
                second.at[pair(h), rows_at(chunk(inner[h], s, small), small)], second_in.at[h, s - 1],
                (2, h, s), inner[h][1][s],
            )
    yield
    if z_out.shape[1] > piece:
        z_out[...] = jnp.zeros(z_out.shape, BF16)
    for h in both:
        for s in (1, 2, 3):
            then[h, s].wait_recv()
        for j in both:
            value = collect(h, j, second, chunk(inner[h], 0, small), small, second_in).astype(BF16)
            for k in both:
                z_out[(2 * h + j) * 2 + k, 0:piece, :] = value[piece * k : piece * (k + 1), :]
    for s in (4, 3, 5, 2, 6, 1, 7):
        send(z_out.at[ring(z, 8, s)], z_in.at[z], z_sems.at[0, 0], z_sems.at[1, 0], zs[s][1], zs[s][0])
    z_in[z] = z_out[z]
    yield
    await_bytes(z_in.at[0:7], z_sems.at[1, 0])
    value = z_in[0].astype(F32)
    for s in range(1, 8):
        value = value + z_in[s].astype(F32)
    z_done[z] = value.astype(BF16)
    for s in (4, 3, 5, 2, 6, 1, 7):
        send(z_done.at[z], z_done.at[z], z_sems.at[0, 1], z_sems.at[1, 1], zs[s][1], zs[s][0])
    yield
    await_bytes(z_done.at[0:7], z_sems.at[1, 1])
    back = {}

    def columns(h):
        return slice(256 * h, 256 * h + 256)

    def share(h, base, axis, size, stage):
        part = total.at[rows_at(base + axis[0] * size, size), columns(h)]
        for s in (2, 1, 3):
            back[stage, h, s] = post(part, part, (stage, h, s), axis[1][s])

    bases = [core * half + chunk(outer[h], 0, large) for h in both]
    for h in both:
        at = bases[h] + chunk(inner[h], 0, small)
        for j in (2 * h, 2 * h + 1):
            joined = jnp.concatenate([z_done[2 * j + k, 0:piece].astype(F32) for k in both], axis=0)
            total[rows_at(at, small), 128 * j : 128 * j + 128] = joined.astype(BF16)
        share(h, bases[h], inner[h], small, 3)
    yield
    for h in both:
        for s in (1, 2, 3):
            back[3, h, s].wait_recv()
        share(h, core * half, outer[h], large, 4)
    last = []

    def to_sibling(h, s):
        part = total.at[rows_at(core * half + chunk(outer[h], -s, large), large), columns(h)]
        last.append(post(part, part, (5, h, s), (x, sibling)))

    for h in both:
        to_sibling(h, 0)
    yield
    for s in (1, 3, 2):
        for h in both:
            back[4, h, s].wait_recv()
            to_sibling(h, s)
    yield
    for copy in last:
        copy.wait_recv()
    await_bytes(z_out.at[0:7], z_sems.at[0, 0])
    await_bytes(z_done.at[0:7], z_sems.at[0, 1])


def gain_reduction(value, result, where, slots, sems):
    x, y, z, core, here, xs, ys, zs = where
    cores = [(x, here), (x, here + 1 - 2 * core)]
    base = 0
    for index, (count, pos, devices) in enumerate(((2, core, cores), (4, x, xs), (4, y, ys), (8, z, zs))):
        slots[base + pos] = value
        for s in range(1, count):
            mine = slots.at[base + pos]
            send(mine, mine, sems.at[0, index], sems.at[1, index], devices[s][1], devices[s][0])
        yield
        await_bytes(slots.at[base : base + count - 1], sems.at[1, index])
        await_bytes(slots.at[base : base + count - 1], sems.at[0, index])
        value = slots[base]
        for s in range(1, count):
            value = value + slots[base + s]
        base += count
    result[...] = value


def advance(step):
    next(step, None)


def layer_kernel(
    nodes, send_rows, senders, receivers, gain, ngain, lat_in, cot_in, ncot_in, w1_in, w2_in, nw1_in, nw2_in,
    edge_grad, node_grad, own_total, table_total, node_total, gain_total,
    lat, cot, ncot, w1, w2, nw1, nw2, others, packed, incoming, far_grad, returned, rim_grad, from_rims,
    onehot, projected, act, slope, hat, scale, raw_grad, pre_grad, node_partial, own_terms, table_terms, node_terms, slots, *rest,
):
    own_scratch, table_scratch, node_scratch = rest[0:10], rest[10:20], rest[20:30]
    load_sems, far_sems, rim_sems, back_sems, back_rim_sems, gain_sems = rest[30:]
    here, x, y, z, core = place()
    edges, width = lat.shape
    count = nodes.shape[0]
    patches = send_rows.shape[1]
    outside = others.shape[0]
    rows = count + outside
    block = 256
    xs = [(x, here)] + [(ring(x, 4, s), here) for s in (1, 2, 3)]
    ys = [(x, here)] + [(x, ring(y, 4, s) * 16 + z * 2 + core) for s in (1, 2, 3)]
    zs = [(x, here)] + [(x, y * 16 + ring(z, 8, s) * 2 + core) for s in range(1, 8)]
    where = (x, y, z, core, here, xs, ys, zs)
    behind, ahead = ring(here, patches, -1), ring(here, patches, 1)

    loads = [
        pltpu.make_async_copy(src, dst, load_sems.at[k])
        for k, (src, dst) in enumerate(
            ((w1_in, w1), (lat_in, lat), (w2_in, w2), (nw1_in, nw1), (nw2_in, nw2), (ncot_in, ncot), (cot_in, cot))
        )
    ]
    for copy in loads:
        copy.start()

    def greet(k, carry):
        signal(lax.rem(here + k, patches), x)
        return carry

    lax.fori_loop(1, patches, greet, 0)
    for s in (1, 2, 3):
        signal(here, ring(x, 4, s))
    spread_nodes = send_one_hot(send_rows[...], count)
    packed[...] = pack(mm_tn(spread_nodes, nodes[...]).astype(BF16), False)
    pl.semaphore_wait(pltpu.get_barrier_semaphore(), patches + 2)
    rims = (
        send(nodes.at[count - RIM : count], others.at[0:RIM], rim_sems.at[0, 0], rim_sems.at[1, 0], ahead, x),
        send(nodes.at[0:RIM], others.at[RIM : 2 * RIM], rim_sems.at[0, 1], rim_sems.at[1, 1], behind, x),
    )

    def push(src, dst, sems):
        def one(k, carry):
            row = lax.rem(y + 2 + k // 2, 4) * 16 + lax.rem(core + k, 2)
            for s in (4, 3, 5, 2, 6, 1, 7, 0):
                to = row + ring(z, 8, s) * 2

                def go():
                    send(src.at[rows_at(to * 16, 16)], dst.at[rows_at(here * 16, 16)], sems.at[0], sems.at[1], to, x)

                if s == 0:
                    pl.when(to != here)(go)
                else:
                    go()
            return carry

        lax.fori_loop(0, patches // 8, one, 0)

    mine = rows_at(here * 16, 16)
    all_but_mine = slice(0, 16 * (patches - 1))
    push(packed, incoming, far_sems)

    send_row, recv_row = senders[...], receivers[...]
    table_row = jnp.where(send_row < RIM, send_row + count, jnp.where(send_row < RIM + count, send_row - RIM, send_row))
    send_col = jnp.transpose(jnp.broadcast_to(table_row, (128, edges)))
    recv_col = jnp.transpose(jnp.broadcast_to(recv_row, (128, edges)))
    onehot[:, 0:count] = one_hot_cols(send_col, count)
    onehot[:, count : 2 * count] = one_hot_cols(recv_col, count)
    onehot[:, 2 * count : 2 * count + outside] = one_hot_cols(send_col, outside, count)
    recv_rows = one_hot_rows(recv_row, count)
    loads[0].wait()
    projected[0:count, :] = mm(nodes[...], w1[width : 2 * width, :]).astype(BF16)
    projected[count : 2 * count, :] = mm(nodes[...], w1[2 * width :, :]).astype(BF16)
    loads[1].wait()
    for start in range(0, edges, block):
        part = slice(start, start + block)
        slope[part, :] = mm(lat[part, :], w1[0:width, :]) + mm(onehot[part, 0 : 2 * count], projected[0 : 2 * count, :])

    for copy in rims:
        copy.wait_recv()
    incoming[mine, :] = packed[mine, :]
    await_bytes(incoming.at[all_but_mine], far_sems.at[1])
    others[2 * RIM :, :] = unpack(incoming[...], True)
    projected[2 * count : 2 * count + outside, :] = mm(others[...], w1[width : 2 * width, :]).astype(BF16)
    loads[2].wait()
    edge_gain = gain[...]
    inflow = jnp.zeros((count, width), F32)
    for start in range(0, edges, block):
        part = slice(start, start + block)
        pre = slope[part, :] + mm(onehot[part, 2 * count :], projected[2 * count :, :])
        sig = jax.nn.sigmoid(pre)
        acted = (pre * sig).astype(BF16)
        act[part, :] = acted
        slope[part, :] = sig * (1.0 + pre * (1.0 - sig))
        normed, inv = normalize(mm(acted, w2[...]))
        hat[part, :] = normed
        scale[part, :] = inv
        inflow = inflow + mm(recv_rows[:, part], (normed * edge_gain).astype(BF16))
    inflow = inflow.astype(BF16)
    for copy in loads[3:]:
        copy.wait()
    node_pre = mm(nodes[...], nw1[0:width, :]) + mm(inflow, nw1[width:, :])
    node_sig = jax.nn.sigmoid(node_pre)
    node_act = (node_pre * node_sig).astype(BF16)
    node_hat, node_scale = normalize(mm(node_act, nw2[...]))
    upstream = ncot[...].astype(F32)
    node_gain_grad = jnp.sum(upstream * node_hat, axis=0, keepdims=True)
    node_raw_grad = normalize_back(upstream * ngain[...], node_hat, node_scale).astype(BF16)
    node_act_grad = mm_nt(node_raw_grad, nw2[...])
    node_pre_grad = (node_act_grad * node_sig * (1.0 + node_pre * (1.0 - node_sig))).astype(BF16)

    def put(terms, row, value):
        for j in range(width // 128):
            terms[j, row : row + value.shape[0], :] = value[:, 128 * j : 128 * j + 128].astype(BF16)

    put(node_terms, 0, mm_tn(nodes[...], node_pre_grad))
    put(node_terms, width, mm_tn(inflow, node_pre_grad))
    put(node_terms, 2 * width, mm_tn(node_act, node_raw_grad))
    pending = []
    node_sum = reduction(node_terms, node_total, where, node_scratch, pending)
    advance(node_sum)
    node_partial[...] = upstream + mm_nt(node_pre_grad, nw1[0:width, :])
    inflow_grad = mm_nt(node_pre_grad, nw1[width:, :]).astype(BF16)
    gain_grad = jnp.zeros((1, width), F32)
    for start in range(0, edges, block):
        part = slice(start, start + block)
        edge_cot = cot[part, :].astype(F32)
        normed = hat[part, :]
        update_grad = edge_cot + mm(onehot[part, count : 2 * count], inflow_grad)
        gain_grad = gain_grad + jnp.sum(update_grad * normed, axis=0, keepdims=True)
        back = normalize_back(update_grad * edge_gain, normed, scale[part, :]).astype(BF16)
        raw_grad[part, :] = back
        pre_back = (mm_nt(back, w2[...]) * slope[part, :]).astype(BF16)
        pre_grad[part, :] = pre_back
        edge_grad[part, :] = (edge_cot + mm_nt(pre_back, w1[0:width, :])).astype(BF16)
        if start == 0:
            advance(node_sum)
    all_pre = pre_grad[...]
    put(own_terms, width, mm_tn(act[...], raw_grad[...]))
    put(own_terms, 0, mm_tn(lat[...], all_pre))
    own_sum = reduction(own_terms, own_total, where, own_scratch, pending)
    advance(own_sum)
    send_sum = mm(one_hot_rows(table_row, rows), all_pre).astype(BF16)
    recv_sum = mm(recv_rows, all_pre).astype(BF16)
    put(table_terms, 0, mm_tn(nodes[...], send_sum[0:count]) + mm_tn(others[...], send_sum[count:]))
    put(table_terms, width, mm_tn(nodes[...], recv_sum))
    table_sum = reduction(table_terms, table_total, where, table_scratch, pending)
    advance(table_sum)
    advance(own_sum)
    gain_rows = [gain_grad[:, 128 * j : 128 * j + 128] for j in range(width // 128)]
    gain_rows += [node_gain_grad[:, 128 * j : 128 * j + 128] for j in range(width // 128)]
    gain_sum = gain_reduction(jnp.concatenate(gain_rows, axis=0), gain_total, where, slots, gain_sems)
    advance(gain_sum)
    other_grad = mm_nt(send_sum[count:], w1[width : 2 * width, :]).astype(BF16)
    rim_grad[...] = other_grad[0 : 2 * RIM]
    back_rims = (
        send(rim_grad.at[RIM : 2 * RIM], from_rims.at[0:RIM], back_rim_sems.at[0, 0], back_rim_sems.at[1, 0], ahead, x),
        send(rim_grad.at[0:RIM], from_rims.at[RIM : 2 * RIM], back_rim_sems.at[0, 1], back_rim_sems.at[1, 1], behind, x),
    )
    advance(table_sum)
    far_grad[...] = pack(other_grad[2 * RIM :], True)
    push(far_grad, returned, back_sems)
    advance(node_sum)
    node_partial[...] += mm_nt(send_sum[0:count], w1[width : 2 * width, :]) + mm_nt(recv_sum, w1[2 * width :, :])
    advance(gain_sum)
    returned[mine, :] = far_grad[mine, :]
    advance(own_sum)
    advance(node_sum)
    advance(table_sum)
    advance(gain_sum)
    advance(own_sum)
    advance(table_sum)
    for copy in back_rims:
        copy.wait_recv()
    await_bytes(returned.at[all_but_mine], back_sems.at[1])
    nodes_done = node_partial[...] + mm(spread_nodes, unpack(returned[...], False))
    node_grad[0:RIM, :] = (nodes_done[0:RIM] + from_rims[0:RIM].astype(F32)).astype(BF16)
    node_grad[RIM : count - RIM, :] = nodes_done[RIM : count - RIM].astype(BF16)
    node_grad[count - RIM : count, :] = (nodes_done[count - RIM :] + from_rims[RIM : 2 * RIM].astype(F32)).astype(BF16)
    advance(gain_sum)
    for step in range(8):
        advance(node_sum)
        advance(own_sum)
        advance(table_sum)
        if step == 1:
            advance(gain_sum)
    for copy in rims + back_rims:
        copy.wait_send()
    await_bytes(packed.at[all_but_mine], far_sems.at[0])
    await_bytes(far_grad.at[all_but_mine], back_sems.at[0])
    for copy in pending:
        copy.wait_send()


def place_kernel(
    own_total, table_total, node_total, edge_in, node_in, gains, first, second, nfirst, nsecond, edge_out, node_out, gain_out, ngain_out, sems
):
    width = first.shape[1]
    copies = [
        pltpu.make_async_copy(src, dst, sems.at[k])
        for k, (src, dst) in enumerate(
            (
                (own_total.at[0:width], first.at[0:width]),
                (table_total, first.at[width : 3 * width]),
                (own_total.at[width : 2 * width], second),
                (node_total.at[0 : 2 * width], nfirst),
                (node_total.at[2 * width : 3 * width], nsecond),
                (edge_in, edge_out),
                (node_in, node_out),
            )
        )
    ]
    for copy in copies:
        copy.start()
    for j in range(width // 128):
        cols = slice(128 * j, 128 * j + 128)
        gain_out[cols] = gains[j, :].astype(BF16)
        ngain_out[cols] = gains[4 + j, :].astype(BF16)
    for copy in copies:
        copy.wait()


def place_results(own_total, table_total, node_total, edge_grad, node_grad, gains):
    width = edge_grad.shape[1]
    anywhere, whole = pl.BlockSpec(memory_space=pl.ANY), pl.BlockSpec(memory_space=VMEM)
    return pl.pallas_call(
        place_kernel,
        out_shape=tuple(
            jax.ShapeDtypeStruct(shape, BF16)
            for shape in (
                (3 * width, width), (width, width), (2 * width, width), (width, width),
                edge_grad.shape, node_grad.shape, (width,), (width,),
            )
        ),
        in_specs=[whole] * 6,
        out_specs=(anywhere,) * 6 + (whole,) * 2,
        scratch_shapes=[pltpu.SemaphoreType.DMA((7,))],
        compiler_params=pltpu.CompilerParams(vmem_limit_bytes=16 * 1024 * 1024),
        name="place_results",
    )(own_total, table_total, node_total, edge_grad, node_grad, gains)


def reduction_scratch(total):
    half = total // 2
    large, small = half // 4, half // 16
    padded = -(-(small // 2) // 16) * 16
    dma = pltpu.SemaphoreType.DMA
    return [
        VMEM((4, half, 128), BF16),
        VMEM((4, half, 128), BF16),
        VMEM((2, 3, 2, large, 128), BF16),
        VMEM((4, large, 128), BF16),
        VMEM((2, 3, 2, small, 128), BF16),
        VMEM((8, padded, 128), BF16),
        VMEM((8, padded, 128), BF16),
        VMEM((8, padded, 128), BF16),
        dma((2, 6, 2, 4)),
        dma((2, 2)),
    ]


def layer(lat, cot, nodes, ncot, senders, receivers, send_rows, w1, w2, gain, nw1, nw2, ngain):
    edges, width = lat.shape
    count = nodes.shape[0]
    patches = send_rows.shape[1]
    outside = 2 * RIM + FAR * patches
    anywhere, whole = pl.BlockSpec(memory_space=pl.ANY), pl.BlockSpec(memory_space=VMEM)
    dma = pltpu.SemaphoreType.DMA
    packed = VMEM((16 * patches, 128), BF16)
    return pl.pallas_call(
        layer_kernel,
        out_shape=(
            VMEM((edges, width), BF16),
            VMEM((count, width), BF16),
            VMEM((2 * width, width), BF16),
            VMEM((2 * width, width), BF16),
            VMEM((3 * width, width), BF16),
            VMEM((8, 128), F32),
        ),
        in_specs=[whole] * 6 + [pl.BlockSpec(memory_space=pltpu.HBM)] * 7,
        out_specs=(whole,) * 6,
        scratch_shapes=[
            VMEM(lat.shape, BF16),
            VMEM(cot.shape, BF16),
            VMEM(ncot.shape, BF16),
            VMEM(w1.shape, BF16),
            VMEM(w2.shape, BF16),
            VMEM(nw1.shape, BF16),
            VMEM(nw2.shape, BF16),
            VMEM((outside, width), BF16),
            packed,
            packed,
            packed,
            packed,
            VMEM((2 * RIM, width), BF16),
            VMEM((2 * RIM, width), BF16),
            VMEM((edges, 2 * count + outside), BF16),
            VMEM((2 * count + outside, width), BF16),
            VMEM((edges, width), BF16),
            VMEM((edges, width), F32),
            VMEM((edges, width), F32),
            VMEM((edges, 1), F32),
            VMEM((edges, width), BF16),
            VMEM((edges, width), BF16),
            VMEM((count, width), F32),
            VMEM((4, 2 * width, 128), BF16),
            VMEM((4, 2 * width, 128), BF16),
            VMEM((4, 3 * width, 128), BF16),
            VMEM((18, 8, 128), F32),
        ]
        + reduction_scratch(2 * width)
        + reduction_scratch(2 * width)
        + reduction_scratch(3 * width)
        + [dma((7,)), dma((2,)), dma((2, 2)), dma((2,)), dma((2, 2)), dma((2, 4))],
        compiler_params=pltpu.CompilerParams(
            collective_id=0, has_side_effects=True, vmem_limit_bytes=56 * 1024 * 1024
        ),
        name="layer",
    )(
        nodes, send_rows, senders.reshape(1, edges), receivers.reshape(1, edges),
        gain.reshape(1, width), ngain.reshape(1, width), lat, cot, ncot, w1, w2, nw1, nw2,
    )


def on_device(
    edge_latents, node_latents, edge_cotangent, node_cotangent, senders, receivers, send_rows,
    edge_first, edge_second, edge_gain, node_first, node_second, node_gain,
):
    width = edge_first.shape[1]
    edge_grad, node_grad, own_total, table_total, node_total, gains = layer(
        edge_latents[0], edge_cotangent[0], node_latents[0], node_cotangent[0], senders, receivers, send_rows.T,
        edge_first, edge_second, edge_gain, node_first, node_second, node_gain,
    )
    first, second, nfirst, nsecond, edge_grad, node_grad, gain_grad, ngain_grad = place_results(
        own_total, table_total, node_total, edge_grad, node_grad, gains
    )
    return (
        edge_grad[None], node_grad[None], first, second, nfirst, nsecond,
        gain_grad, ngain_grad,
    )


def solution(mesh):
    return jax.shard_map(
        on_device,
        mesh=mesh,
        in_specs=(
            P("sample", "patch", None), P("sample", "patch", None), P("sample", "patch", None),
            P("sample", "patch", None), P("patch"), P("patch"), P("patch", None),
            P(), P(), P(), P(), P(), P(),
        ),
        out_specs=(P("sample", "patch", None), P("sample", "patch", None), P(), P(), P(), P(), P(), P()),
        check_vma=False,
    )
```

```python
import functools

import jax
import jax.numpy as jnp
from jax import lax
from jax.experimental import pallas as pl
from jax.experimental.pallas import tpu as pltpu
from jax.sharding import PartitionSpec as P

RIM = 32
FAR = 4
MESH = pl.DeviceIdType.MESH
F32 = jnp.float32
BF16 = jnp.bfloat16
VMEM = pltpu.VMEM


def mm(a, b):
    return lax.dot_general(a, b, (((1,), (0,)), ((), ())), preferred_element_type=F32)


def mm_nt(a, b):
    return lax.dot_general(a, b, (((1,), (1,)), ((), ())), preferred_element_type=F32)


def mm_tn(a, b):
    return lax.dot_general(a, b, (((0,), (0,)), ((), ())), preferred_element_type=F32)


def one_hot_cols(col, width, first=0):
    parts = []
    lanes = lax.broadcasted_iota(jnp.int32, col.shape, 1) + first
    for start in range(0, width, 128):
        size = min(128, width - start)
        hit = (col == lanes + start).astype(F32).astype(BF16)
        parts.append(hit if size == 128 else hit[:, :size])
    return jnp.concatenate(parts, axis=1) if len(parts) > 1 else parts[0]


def one_hot_rows(row, height):
    ids = lax.broadcasted_iota(jnp.int32, (height, row.shape[1]), 0)
    return (ids == row).astype(F32).astype(BF16)


def lane_block(packed, c):
    return (lax.broadcasted_iota(jnp.int32, packed.shape, 0) // FAR) % 4 == c


def spread(rows, by_patch):
    at = lax.broadcasted_iota(jnp.int32, (4 * rows, rows), 0)
    col = lax.broadcasted_iota(jnp.int32, (4 * rows, rows), 1)
    patch, r = at // 16, at % 4
    return (col == (patch * FAR + r if by_patch else r * (rows // FAR) + patch)).astype(F32).astype(BF16)


def unspread(rows, by_patch):
    at = lax.broadcasted_iota(jnp.int32, (rows, 4 * rows), 1)
    row = lax.broadcasted_iota(jnp.int32, (rows, 4 * rows), 0)
    patch, r = at // 16, at % 4
    return (row == (patch * FAR + r if by_patch else r * (rows // FAR) + patch)).astype(F32).astype(BF16)


def pack(values, by_patch):
    wide = mm(spread(values.shape[0], by_patch), values)
    packed = wide[:, 0:128]
    for c in (1, 2, 3):
        packed = jnp.where(lane_block(packed, c), wide[:, 128 * c : 128 * c + 128], packed)
    return packed.astype(BF16)


def unpack(packed, by_patch):
    values = packed.astype(F32)
    wide = jnp.concatenate([jnp.where(lane_block(values, c), values, 0.0).astype(BF16) for c in range(4)], axis=1)
    return mm(unspread(packed.shape[0] // 4, by_patch), wide).astype(BF16)


def send_one_hot(send_rows, count):
    return jnp.concatenate([one_hot_rows(send_rows[r : r + 1, :], count) for r in range(FAR)], axis=1)


def normalize(values):
    center = values - jnp.mean(values, axis=1, keepdims=True)
    spread = jnp.mean(center * center, axis=1, keepdims=True)
    scale = lax.rsqrt(spread + 1e-05)
    return (center * scale, scale)


def normalize_back(grads, normed, scale):
    first = jnp.mean(grads, axis=1, keepdims=True)
    second = jnp.mean(grads * normed, axis=1, keepdims=True)
    return (grads - first - normed * second) * scale


def place():
    here = lax.axis_index("patch")
    return here, lax.axis_index("sample"), lax.div(here, 16), lax.rem(lax.div(here, 2), 8), lax.rem(here, 2)


def ring(here, count, step):
    return lax.rem(here + (step + count) % count, count)


def signal(patch, sample):
    pl.semaphore_signal(
        pltpu.get_barrier_semaphore(), inc=1, device_id={"patch": patch, "sample": sample}, device_id_type=MESH
    )


def send(src, dst, send_sem, recv_sem, patch, sample):
    copy = pltpu.make_async_remote_copy(
        src_ref=src, dst_ref=dst, send_sem=send_sem, recv_sem=recv_sem,
        device_id={"patch": patch, "sample": sample}, device_id_type=MESH,
    )
    copy.start()
    return copy


def await_bytes(ref, sem):
    pltpu.make_async_copy(ref, ref, sem).wait()


def rows_at(start, size, align=16):
    return pl.ds(pl.multiple_of(start, align), size)


def reduction(terms, total, where, scratch, pending):
    x, y, z, core, here, xs, ys, zs = where
    core_in, summed, first_in, second, second_in, z_out, z_in, z_done, sems, z_sems = scratch
    half = terms.shape[1] // 2
    large, small = half // 4, half // 16
    piece = small // 2
    sibling = here + 1 - 2 * core
    outer = ((x, xs), (y, ys))
    inner = ((y, ys), (x, xs))
    both = (0, 1)

    def post(src, dst, index, device):
        copy = send(src, dst, sems.at[(0,) + index], sems.at[(1,) + index], device[1], device[0])
        pending.append(copy)
        return copy

    def pair(h):
        return slice(2 * h, 2 * h + 2)

    def chunk(axis, s, size):
        return ring(axis[0], 4, s) * size

    copies = {}
    for k, s in enumerate((2, 1, 3, 0)):
        for h in both:
            at = chunk(outer[h], s, large)
            copies[h, s] = post(
                terms.at[pair(h), rows_at((1 - core) * half + at, large)],
                core_in.at[pair(h), rows_at(at, large)], (0, h, s), (x, sibling),
            )
    yield

    def core_ready(h, s):
        copies[h, s].wait_recv()
        at = chunk(outer[h], s, large)
        for j in (2 * h, 2 * h + 1):
            mine = terms[j, rows_at(core * half + at, large)].astype(F32)
            summed[j, rows_at(at, large)] = (mine + core_in[j, rows_at(at, large)].astype(F32)).astype(BF16)

    first = {}
    for s in (2, 1, 3):
        for h in both:
            core_ready(h, s)
            first[h, s] = post(
                summed.at[pair(h), rows_at(chunk(outer[h], s, large), large)], first_in.at[h, s - 1],
                (1, h, s), outer[h][1][s],
            )
    for h in both:
        core_ready(h, 0)
    yield

    def collect(h, j, source, at, size, landing):
        value = source[2 * h + j, rows_at(at, size)].astype(F32)
        for s in (1, 2, 3):
            value = value + landing[h, s - 1, j].astype(F32)
        return value

    then = {}
    for h in both:
        for s in (1, 2, 3):
            first[h, s].wait_recv()
        for j in both:
            second[2 * h + j] = collect(h, j, summed, chunk(outer[h], 0, large), large, first_in).astype(BF16)
        for s in (2, 1, 3):
            then[h, s] = post(
                second.at[pair(h), rows_at(chunk(inner[h], s, small), small)], second_in.at[h, s - 1],
                (2, h, s), inner[h][1][s],
            )
    yield
    if z_out.shape[1] > piece:
        z_out[...] = jnp.zeros(z_out.shape, BF16)
    for h in both:
        for s in (1, 2, 3):
            then[h, s].wait_recv()
        for j in both:
            value = collect(h, j, second, chunk(inner[h], 0, small), small, second_in).astype(BF16)
            for k in both:
                z_out[(2 * h + j) * 2 + k, 0:piece, :] = value[piece * k : piece * (k + 1), :]
    for s in (4, 3, 5, 2, 6, 1, 7):
        send(z_out.at[ring(z, 8, s)], z_in.at[z], z_sems.at[0, 0], z_sems.at[1, 0], zs[s][1], zs[s][0])
    z_in[z] = z_out[z]
    yield
    await_bytes(z_in.at[0:7], z_sems.at[1, 0])
    value = z_in[0].astype(F32)
    for s in range(1, 8):
        value = value + z_in[s].astype(F32)
    z_done[z] = value.astype(BF16)
    for s in (4, 3, 5, 2, 6, 1, 7):
        send(z_done.at[z], z_done.at[z], z_sems.at[0, 1], z_sems.at[1, 1], zs[s][1], zs[s][0])
    yield
    await_bytes(z_done.at[0:7], z_sems.at[1, 1])
    back = {}

    def columns(h):
        return slice(256 * h, 256 * h + 256)

    def share(h, base, axis, size, stage):
        part = total.at[rows_at(base + axis[0] * size, size), columns(h)]
        for s in (2, 1, 3):
            back[stage, h, s] = post(part, part, (stage, h, s), axis[1][s])

    bases = [core * half + chunk(outer[h], 0, large) for h in both]
    for h in both:
        at = bases[h] + chunk(inner[h], 0, small)
        for j in (2 * h, 2 * h + 1):
            joined = jnp.concatenate([z_done[2 * j + k, 0:piece].astype(F32) for k in both], axis=0)
            total[rows_at(at, small), 128 * j : 128 * j + 128] = joined.astype(BF16)
        share(h, bases[h], inner[h], small, 3)
    yield
    for h in both:
        for s in (1, 2, 3):
            back[3, h, s].wait_recv()
        share(h, core * half, outer[h], large, 4)
    last = []

    def to_sibling(h, s):
        part = total.at[rows_at(core * half + chunk(outer[h], -s, large), large), columns(h)]
        last.append(post(part, part, (5, h, s), (x, sibling)))

    for h in both:
        to_sibling(h, 0)
    yield
    for s in (1, 3, 2):
        for h in both:
            back[4, h, s].wait_recv()
            to_sibling(h, s)
    yield
    for copy in last:
        copy.wait_recv()
    await_bytes(z_out.at[0:7], z_sems.at[0, 0])
    await_bytes(z_done.at[0:7], z_sems.at[0, 1])


def gain_reduction(value, result, where, slots, sems):
    x, y, z, core, here, xs, ys, zs = where
    cores = [(x, here), (x, here + 1 - 2 * core)]
    base = 0
    for index, (count, pos, devices) in enumerate(((2, core, cores), (4, x, xs), (4, y, ys), (8, z, zs))):
        slots[base + pos] = value
        for s in range(1, count):
            mine = slots.at[base + pos]
            send(mine, mine, sems.at[0, index], sems.at[1, index], devices[s][1], devices[s][0])
        yield
        await_bytes(slots.at[base : base + count - 1], sems.at[1, index])
        await_bytes(slots.at[base : base + count - 1], sems.at[0, index])
        value = slots[base]
        for s in range(1, count):
            value = value + slots[base + s]
        base += count
    result[...] = value


def advance(step):
    next(step, None)


def layer_kernel(
    nodes_in, send_rows, senders, receivers, gain, ngain, lat_in, cot_in, ncot_in, w1_in, w2_in, nw1_in, nw2_in,
    edge_grad, node_grad, own_total, table_total, node_total, gain_total,
    nodes, lat, cot, ncot, w1, w2, nw1, nw2, others, packed, incoming, far_grad, returned, rim_grad, from_rims,
    onehot, projected, act, slope, hat, scale, raw_grad, pre_grad, node_partial, own_terms, table_terms, node_terms, slots, *rest,
):
    own_scratch, table_scratch, node_scratch = rest[0:10], rest[10:20], rest[20:30]
    load_sems, far_sems, rim_sems, back_sems, back_rim_sems, gain_sems = rest[30:]
    here, x, y, z, core = place()
    edges, width = lat.shape
    count = nodes.shape[0]
    patches = send_rows.shape[1]
    outside = others.shape[0]
    rows = count + outside
    block = 256
    xs = [(x, here)] + [(ring(x, 4, s), here) for s in (1, 2, 3)]
    ys = [(x, here)] + [(x, ring(y, 4, s) * 16 + z * 2 + core) for s in (1, 2, 3)]
    zs = [(x, here)] + [(x, y * 16 + ring(z, 8, s) * 2 + core) for s in range(1, 8)]
    where = (x, y, z, core, here, xs, ys, zs)
    behind, ahead = ring(here, patches, -1), ring(here, patches, 1)

    loads = [
        pltpu.make_async_copy(src, dst, load_sems.at[k])
        for k, (src, dst) in enumerate(
            (
                (nodes_in, nodes), (w1_in, w1), (lat_in, lat), (w2_in, w2),
                (nw1_in, nw1), (nw2_in, nw2), (ncot_in, ncot), (cot_in, cot),
            )
        )
    ]
    for copy in loads:
        copy.start()

    def greet(k, carry):
        signal(lax.rem(here + k, patches), x)
        return carry

    lax.fori_loop(1, patches, greet, 0)
    for s in (1, 2, 3):
        signal(here, ring(x, 4, s))
    spread_nodes = send_one_hot(send_rows[...], count)
    loads[0].wait()
    packed[...] = pack(mm_tn(spread_nodes, nodes[...]).astype(BF16), False)
    pl.semaphore_wait(pltpu.get_barrier_semaphore(), patches + 2)
    rims = (
        send(nodes.at[count - RIM : count], others.at[0:RIM], rim_sems.at[0, 0], rim_sems.at[1, 0], ahead, x),
        send(nodes.at[0:RIM], others.at[RIM : 2 * RIM], rim_sems.at[0, 1], rim_sems.at[1, 1], behind, x),
    )

    def push(src, dst, sems, first, last):
        def one(k, carry):
            row = lax.rem(y + 2 + k // 2, 4) * 16 + lax.rem(core + k, 2)
            for s in (4, 3, 5, 2, 6, 1, 7, 0):
                to = row + ring(z, 8, s) * 2

                def go():
                    send(src.at[rows_at(to * 16, 16)], dst.at[rows_at(here * 16, 16)], sems.at[0], sems.at[1], to, x)

                if s == 0:
                    pl.when(to != here)(go)
                else:
                    go()
            return carry

        lax.fori_loop(first, last, one, 0)

    mine = rows_at(here * 16, 16)
    all_but_mine = slice(0, 16 * (patches - 1))
    push(packed, incoming, far_sems, 0, patches // 8)

    send_row, recv_row = senders[...], receivers[...]
    table_row = jnp.where(send_row < RIM, send_row + count, jnp.where(send_row < RIM + count, send_row - RIM, send_row))
    send_col = jnp.transpose(jnp.broadcast_to(table_row, (128, edges)))
    recv_col = jnp.transpose(jnp.broadcast_to(recv_row, (128, edges)))
    onehot[:, 0:count] = one_hot_cols(send_col, count)
    onehot[:, count : 2 * count] = one_hot_cols(recv_col, count)
    onehot[:, 2 * count : 2 * count + outside] = one_hot_cols(send_col, outside, count)
    recv_rows = one_hot_rows(recv_row, count)
    loads[1].wait()
    projected[0:count, :] = mm(nodes[...], w1[width : 2 * width, :]).astype(BF16)
    projected[count : 2 * count, :] = mm(nodes[...], w1[2 * width :, :]).astype(BF16)
    loads[2].wait()
    for start in range(0, edges, block):
        part = slice(start, start + block)
        slope[part, :] = mm(lat[part, :], w1[0:width, :]) + mm(onehot[part, 0 : 2 * count], projected[0 : 2 * count, :])

    for copy in rims:
        copy.wait_recv()
    incoming[mine, :] = packed[mine, :]
    await_bytes(incoming.at[all_but_mine], far_sems.at[1])
    others[2 * RIM :, :] = unpack(incoming[...], True)
    projected[2 * count : 2 * count + outside, :] = mm(others[...], w1[width : 2 * width, :]).astype(BF16)
    loads[3].wait()
    edge_gain = gain[...]
    inflow = jnp.zeros((count, width), F32)
    for start in range(0, edges, block):
        part = slice(start, start + block)
        pre = slope[part, :] + mm(onehot[part, 2 * count :], projected[2 * count :, :])
        sig = jax.nn.sigmoid(pre)
        acted = (pre * sig).astype(BF16)
        act[part, :] = acted
        slope[part, :] = sig * (1.0 + pre * (1.0 - sig))
        normed, inv = normalize(mm(acted, w2[...]))
        hat[part, :] = normed
        scale[part, :] = inv
        inflow = inflow + mm(recv_rows[:, part], (normed * edge_gain).astype(BF16))
    inflow = inflow.astype(BF16)
    for copy in loads[4:]:
        copy.wait()
    node_pre = mm(nodes[...], nw1[0:width, :]) + mm(inflow, nw1[width:, :])
    node_sig = jax.nn.sigmoid(node_pre)
    node_act = (node_pre * node_sig).astype(BF16)
    node_hat, node_scale = normalize(mm(node_act, nw2[...]))
    upstream = ncot[...].astype(F32)
    node_gain_grad = jnp.sum(upstream * node_hat, axis=0, keepdims=True)
    node_raw_grad = normalize_back(upstream * ngain[...], node_hat, node_scale).astype(BF16)
    node_act_grad = mm_nt(node_raw_grad, nw2[...])
    node_pre_grad = (node_act_grad * node_sig * (1.0 + node_pre * (1.0 - node_sig))).astype(BF16)

    def put(terms, row, value):
        for j in range(width // 128):
            terms[j, row : row + value.shape[0], :] = value[:, 128 * j : 128 * j + 128].astype(BF16)

    put(node_terms, 0, mm_tn(nodes[...], node_pre_grad))
    put(node_terms, width, mm_tn(inflow, node_pre_grad))
    put(node_terms, 2 * width, mm_tn(node_act, node_raw_grad))
    pending = []
    node_sum = reduction(node_terms, node_total, where, node_scratch, pending)
    advance(node_sum)
    node_partial[...] = upstream + mm_nt(node_pre_grad, nw1[0:width, :])
    inflow_grad = mm_nt(node_pre_grad, nw1[width:, :]).astype(BF16)
    gain_grad = jnp.zeros((1, width), F32)
    for start in range(0, edges, block):
        part = slice(start, start + block)
        edge_cot = cot[part, :].astype(F32)
        normed = hat[part, :]
        update_grad = edge_cot + mm(onehot[part, count : 2 * count], inflow_grad)
        gain_grad = gain_grad + jnp.sum(update_grad * normed, axis=0, keepdims=True)
        back = normalize_back(update_grad * edge_gain, normed, scale[part, :]).astype(BF16)
        raw_grad[part, :] = back
        pre_back = (mm_nt(back, w2[...]) * slope[part, :]).astype(BF16)
        pre_grad[part, :] = pre_back
        edge_grad[part, :] = (edge_cot + mm_nt(pre_back, w1[0:width, :])).astype(BF16)
        if start == 0:
            advance(node_sum)
    all_pre = pre_grad[...]
    put(own_terms, width, mm_tn(act[...], raw_grad[...]))
    put(own_terms, 0, mm_tn(lat[...], all_pre))
    own_sum = reduction(own_terms, own_total, where, own_scratch, pending)
    advance(own_sum)
    send_sum = mm(one_hot_rows(table_row, rows), all_pre).astype(BF16)
    recv_sum = mm(recv_rows, all_pre).astype(BF16)
    put(table_terms, 0, mm_tn(nodes[...], send_sum[0:count]) + mm_tn(others[...], send_sum[count:]))
    put(table_terms, width, mm_tn(nodes[...], recv_sum))
    table_sum = reduction(table_terms, table_total, where, table_scratch, pending)
    advance(table_sum)
    advance(own_sum)
    gain_rows = [gain_grad[:, 128 * j : 128 * j + 128] for j in range(width // 128)]
    gain_rows += [node_gain_grad[:, 128 * j : 128 * j + 128] for j in range(width // 128)]
    gain_sum = gain_reduction(jnp.concatenate(gain_rows, axis=0), gain_total, where, slots, gain_sems)
    advance(gain_sum)
    other_grad = mm_nt(send_sum[count:], w1[width : 2 * width, :]).astype(BF16)
    rim_grad[...] = other_grad[0 : 2 * RIM]
    back_rims = (
        send(rim_grad.at[RIM : 2 * RIM], from_rims.at[0:RIM], back_rim_sems.at[0, 0], back_rim_sems.at[1, 0], ahead, x),
        send(rim_grad.at[0:RIM], from_rims.at[RIM : 2 * RIM], back_rim_sems.at[0, 1], back_rim_sems.at[1, 1], behind, x),
    )
    advance(table_sum)
    advance(node_sum)
    far_grad[...] = pack(other_grad[2 * RIM :], True)
    node_partial[...] += mm_nt(send_sum[0:count], w1[width : 2 * width, :]) + mm_nt(recv_sum, w1[2 * width :, :])
    advance(gain_sum)
    returned[mine, :] = far_grad[mine, :]
    for step in (own_sum, node_sum, table_sum, gain_sum, own_sum, table_sum, node_sum):
        advance(step)
    parts = patches // 8
    turns = (own_sum, table_sum, node_sum, own_sum, table_sum, node_sum, own_sum, table_sum)
    for k, step in enumerate(turns):
        push(far_grad, returned, back_sems, parts * k // 8, parts * (k + 1) // 8)
        advance(step)
        if k == 4:
            advance(gain_sum)
    advance(gain_sum)
    advance(node_sum)
    for copy in back_rims:
        copy.wait_recv()
    await_bytes(returned.at[all_but_mine], back_sems.at[1])
    nodes_done = node_partial[...] + mm(spread_nodes, unpack(returned[...], False))
    node_grad[0:RIM, :] = (nodes_done[0:RIM] + from_rims[0:RIM].astype(F32)).astype(BF16)
    node_grad[RIM : count - RIM, :] = nodes_done[RIM : count - RIM].astype(BF16)
    node_grad[count - RIM : count, :] = (nodes_done[count - RIM :] + from_rims[RIM : 2 * RIM].astype(F32)).astype(BF16)
    for _ in (0, 1):
        advance(own_sum)
        advance(table_sum)
        advance(node_sum)
    for copy in rims + back_rims:
        copy.wait_send()
    await_bytes(packed.at[all_but_mine], far_sems.at[0])
    await_bytes(far_grad.at[all_but_mine], back_sems.at[0])
    for copy in pending:
        copy.wait_send()


def place_kernel(
    own_total, table_total, node_total, edge_in, node_in, gains, first, second, nfirst, nsecond, edge_out, node_out, gain_out, ngain_out, sems
):
    width = first.shape[1]
    copies = [
        pltpu.make_async_copy(src, dst, sems.at[k])
        for k, (src, dst) in enumerate(
            (
                (own_total.at[0:width], first.at[0:width]),
                (table_total, first.at[width : 3 * width]),
                (own_total.at[width : 2 * width], second),
                (node_total.at[0 : 2 * width], nfirst),
                (node_total.at[2 * width : 3 * width], nsecond),
                (edge_in, edge_out),
                (node_in, node_out),
            )
        )
    ]
    for copy in copies:
        copy.start()
    for j in range(width // 128):
        cols = slice(128 * j, 128 * j + 128)
        gain_out[cols] = gains[j, :].astype(BF16)
        ngain_out[cols] = gains[4 + j, :].astype(BF16)
    for copy in copies:
        copy.wait()


def place_results(own_total, table_total, node_total, edge_grad, node_grad, gains):
    width = edge_grad.shape[1]
    anywhere, whole = pl.BlockSpec(memory_space=pl.ANY), pl.BlockSpec(memory_space=VMEM)
    return pl.pallas_call(
        place_kernel,
        out_shape=tuple(
            jax.ShapeDtypeStruct(shape, BF16)
            for shape in (
                (3 * width, width), (width, width), (2 * width, width), (width, width),
                edge_grad.shape, node_grad.shape, (width,), (width,),
            )
        ),
        in_specs=[whole] * 6,
        out_specs=(anywhere,) * 6 + (whole,) * 2,
        scratch_shapes=[pltpu.SemaphoreType.DMA((7,))],
        compiler_params=pltpu.CompilerParams(vmem_limit_bytes=16 * 1024 * 1024),
        name="place_results",
    )(own_total, table_total, node_total, edge_grad, node_grad, gains)


def reduction_scratch(total):
    half = total // 2
    large, small = half // 4, half // 16
    padded = -(-(small // 2) // 16) * 16
    dma = pltpu.SemaphoreType.DMA
    return [
        VMEM((4, half, 128), BF16),
        VMEM((4, half, 128), BF16),
        VMEM((2, 3, 2, large, 128), BF16),
        VMEM((4, large, 128), BF16),
        VMEM((2, 3, 2, small, 128), BF16),
        VMEM((8, padded, 128), BF16),
        VMEM((8, padded, 128), BF16),
        VMEM((8, padded, 128), BF16),
        dma((2, 6, 2, 4)),
        dma((2, 2)),
    ]


def layer(lat, cot, nodes, ncot, senders, receivers, send_rows, w1, w2, gain, nw1, nw2, ngain):
    edges, width = lat.shape
    count = nodes.shape[0]
    patches = send_rows.shape[1]
    outside = 2 * RIM + FAR * patches
    anywhere, whole = pl.BlockSpec(memory_space=pl.ANY), pl.BlockSpec(memory_space=VMEM)
    dma = pltpu.SemaphoreType.DMA
    packed = VMEM((16 * patches, 128), BF16)
    return pl.pallas_call(
        layer_kernel,
        out_shape=(
            VMEM((edges, width), BF16),
            VMEM((count, width), BF16),
            VMEM((2 * width, width), BF16),
            VMEM((2 * width, width), BF16),
            VMEM((3 * width, width), BF16),
            VMEM((8, 128), F32),
        ),
        in_specs=[anywhere] + [whole] * 5 + [anywhere] * 7,
        out_specs=(whole,) * 6,
        scratch_shapes=[
            VMEM(nodes.shape, BF16),
            VMEM(lat.shape, BF16),
            VMEM(cot.shape, BF16),
            VMEM(ncot.shape, BF16),
            VMEM(w1.shape, BF16),
            VMEM(w2.shape, BF16),
            VMEM(nw1.shape, BF16),
            VMEM(nw2.shape, BF16),
            VMEM((outside, width), BF16),
            packed,
            packed,
            packed,
            packed,
            VMEM((2 * RIM, width), BF16),
            VMEM((2 * RIM, width), BF16),
            VMEM((edges, 2 * count + outside), BF16),
            VMEM((2 * count + outside, width), BF16),
            VMEM((edges, width), BF16),
            VMEM((edges, width), F32),
            VMEM((edges, width), F32),
            VMEM((edges, 1), F32),
            VMEM((edges, width), BF16),
            VMEM((edges, width), BF16),
            VMEM((count, width), F32),
            VMEM((4, 2 * width, 128), BF16),
            VMEM((4, 2 * width, 128), BF16),
            VMEM((4, 3 * width, 128), BF16),
            VMEM((18, 8, 128), F32),
        ]
        + reduction_scratch(2 * width)
        + reduction_scratch(2 * width)
        + reduction_scratch(3 * width)
        + [dma((8,)), dma((2,)), dma((2, 2)), dma((2,)), dma((2, 2)), dma((2, 4))],
        compiler_params=pltpu.CompilerParams(
            collective_id=0, has_side_effects=True, vmem_limit_bytes=56 * 1024 * 1024
        ),
        name="layer",
    )(
        nodes, send_rows, senders.reshape(1, edges), receivers.reshape(1, edges),
        gain.reshape(1, width), ngain.reshape(1, width), lat, cot, ncot, w1, w2, nw1, nw2,
    )


def on_device(
    edge_latents, node_latents, edge_cotangent, node_cotangent, senders, receivers, send_rows,
    edge_first, edge_second, edge_gain, node_first, node_second, node_gain,
):
    width = edge_first.shape[1]
    edge_grad, node_grad, own_total, table_total, node_total, gains = layer(
        edge_latents[0], edge_cotangent[0], node_latents[0], node_cotangent[0], senders, receivers, send_rows.T,
        edge_first, edge_second, edge_gain, node_first, node_second, node_gain,
    )
    first, second, nfirst, nsecond, edge_grad, node_grad, gain_grad, ngain_grad = place_results(
        own_total, table_total, node_total, edge_grad, node_grad, gains
    )
    return (
        edge_grad[None], node_grad[None], first, second, nfirst, nsecond,
        gain_grad, ngain_grad,
    )


def solution(mesh):
    return jax.shard_map(
        on_device,
        mesh=mesh,
        in_specs=(
            P("sample", "patch", None), P("sample", "patch", None), P("sample", "patch", None),
            P("sample", "patch", None), P("patch"), P("patch"), P("patch", None),
            P(), P(), P(), P(), P(), P(),
        ),
        out_specs=(P("sample", "patch", None), P("sample", "patch", None), P(), P(), P(), P(), P(), P()),
        check_vma=False,
    )
```

```python
import functools

import jax
import jax.numpy as jnp
from jax import lax
from jax.experimental import pallas as pl
from jax.experimental.pallas import tpu as pltpu
from jax.sharding import PartitionSpec as P

RIM = 32
FAR = 4
MESH = pl.DeviceIdType.MESH
F32 = jnp.float32
BF16 = jnp.bfloat16
VMEM = pltpu.VMEM


def mm(a, b):
    return lax.dot_general(a, b, (((1,), (0,)), ((), ())), preferred_element_type=F32)


def mm_nt(a, b):
    return lax.dot_general(a, b, (((1,), (1,)), ((), ())), preferred_element_type=F32)


def mm_tn(a, b):
    return lax.dot_general(a, b, (((0,), (0,)), ((), ())), preferred_element_type=F32)


def one_hot_cols(col, width, first=0):
    parts = []
    lanes = lax.broadcasted_iota(jnp.int32, col.shape, 1) + first
    for start in range(0, width, 128):
        size = min(128, width - start)
        hit = (col == lanes + start).astype(F32).astype(BF16)
        parts.append(hit if size == 128 else hit[:, :size])
    return jnp.concatenate(parts, axis=1) if len(parts) > 1 else parts[0]


def one_hot_rows(row, height):
    ids = lax.broadcasted_iota(jnp.int32, (height, row.shape[1]), 0)
    return (ids == row).astype(F32).astype(BF16)


def lane_block(packed, c):
    return (lax.broadcasted_iota(jnp.int32, packed.shape, 0) // FAR) % 4 == c


def spread(rows, by_patch):
    at = lax.broadcasted_iota(jnp.int32, (4 * rows, rows), 0)
    col = lax.broadcasted_iota(jnp.int32, (4 * rows, rows), 1)
    patch, r = at // 16, at % 4
    return (col == (patch * FAR + r if by_patch else r * (rows // FAR) + patch)).astype(F32).astype(BF16)


def unspread(rows, by_patch):
    at = lax.broadcasted_iota(jnp.int32, (rows, 4 * rows), 1)
    row = lax.broadcasted_iota(jnp.int32, (rows, 4 * rows), 0)
    patch, r = at // 16, at % 4
    return (row == (patch * FAR + r if by_patch else r * (rows // FAR) + patch)).astype(F32).astype(BF16)


def pack(values, by_patch):
    wide = mm(spread(values.shape[0], by_patch), values)
    packed = wide[:, 0:128]
    for c in (1, 2, 3):
        packed = jnp.where(lane_block(packed, c), wide[:, 128 * c : 128 * c + 128], packed)
    return packed.astype(BF16)


def unpack(packed, by_patch):
    values = packed.astype(F32)
    wide = jnp.concatenate([jnp.where(lane_block(values, c), values, 0.0).astype(BF16) for c in range(4)], axis=1)
    return mm(unspread(packed.shape[0] // 4, by_patch), wide).astype(BF16)


def send_one_hot(send_rows, count):
    return jnp.concatenate([one_hot_rows(send_rows[r : r + 1, :], count) for r in range(FAR)], axis=1)


def normalize(values):
    center = values - jnp.mean(values, axis=1, keepdims=True)
    spread = jnp.mean(center * center, axis=1, keepdims=True)
    scale = lax.rsqrt(spread + 1e-05)
    return (center * scale, scale)


def normalize_back(grads, normed, scale):
    first = jnp.mean(grads, axis=1, keepdims=True)
    second = jnp.mean(grads * normed, axis=1, keepdims=True)
    return (grads - first - normed * second) * scale


def place():
    here = lax.axis_index("patch")
    return here, lax.axis_index("sample"), lax.div(here, 16), lax.rem(lax.div(here, 2), 8), lax.rem(here, 2)


def ring(here, count, step):
    return lax.rem(here + (step + count) % count, count)


def signal(patch, sample):
    pl.semaphore_signal(
        pltpu.get_barrier_semaphore(), inc=1, device_id={"patch": patch, "sample": sample}, device_id_type=MESH
    )


def send(src, dst, send_sem, recv_sem, patch, sample):
    copy = pltpu.make_async_remote_copy(
        src_ref=src, dst_ref=dst, send_sem=send_sem, recv_sem=recv_sem,
        device_id={"patch": patch, "sample": sample}, device_id_type=MESH,
    )
    copy.start()
    return copy


def await_bytes(ref, sem):
    pltpu.make_async_copy(ref, ref, sem).wait()


def rows_at(start, size, align=16):
    return pl.ds(pl.multiple_of(start, align), size)


def reduction(terms, total, where, scratch, pending):
    x, y, z, core, here, xs, ys, zs = where
    core_in, summed, first_in, second, second_in, z_out, z_in, z_done, sems, z_sems = scratch
    half = terms.shape[1] // 2
    large, small = half // 4, half // 16
    piece = small // 2
    sibling = here + 1 - 2 * core
    outer = ((x, xs), (y, ys))
    inner = ((y, ys), (x, xs))
    both = (0, 1)

    def post(src, dst, index, device):
        copy = send(src, dst, sems.at[(0,) + index], sems.at[(1,) + index], device[1], device[0])
        pending.append(copy)
        return copy

    def pair(h):
        return slice(2 * h, 2 * h + 2)

    def chunk(axis, s, size):
        return ring(axis[0], 4, s) * size

    copies = {}
    for k, s in enumerate((2, 1, 3, 0)):
        for h in both:
            at = chunk(outer[h], s, large)
            copies[h, s] = post(
                terms.at[pair(h), rows_at((1 - core) * half + at, large)],
                core_in.at[pair(h), rows_at(at, large)], (0, h, s), (x, sibling),
            )
    yield

    def core_ready(h, s):
        copies[h, s].wait_recv()
        at = chunk(outer[h], s, large)
        for j in (2 * h, 2 * h + 1):
            mine = terms[j, rows_at(core * half + at, large)].astype(F32)
            summed[j, rows_at(at, large)] = (mine + core_in[j, rows_at(at, large)].astype(F32)).astype(BF16)

    first = {}
    for s in (2, 1, 3):
        for h in both:
            core_ready(h, s)
            first[h, s] = post(
                summed.at[pair(h), rows_at(chunk(outer[h], s, large), large)], first_in.at[h, s - 1],
                (1, h, s), outer[h][1][s],
            )
    for h in both:
        core_ready(h, 0)
    yield

    def collect(h, j, source, at, size, landing):
        value = source[2 * h + j, rows_at(at, size)].astype(F32)
        for s in (1, 2, 3):
            value = value + landing[h, s - 1, j].astype(F32)
        return value

    then = {}
    for h in both:
        for s in (1, 2, 3):
            first[h, s].wait_recv()
        for j in both:
            second[2 * h + j] = collect(h, j, summed, chunk(outer[h], 0, large), large, first_in).astype(BF16)
        for s in (2, 1, 3):
            then[h, s] = post(
                second.at[pair(h), rows_at(chunk(inner[h], s, small), small)], second_in.at[h, s - 1],
                (2, h, s), inner[h][1][s],
            )
    yield
    if z_out.shape[1] > piece:
        z_out[...] = jnp.zeros(z_out.shape, BF16)
    for h in both:
        for s in (1, 2, 3):
            then[h, s].wait_recv()
        for j in both:
            value = collect(h, j, second, chunk(inner[h], 0, small), small, second_in).astype(BF16)
            for k in both:
                z_out[(2 * h + j) * 2 + k, 0:piece, :] = value[piece * k : piece * (k + 1), :]
    for s in (4, 3, 5, 2, 6, 1, 7):
        send(z_out.at[ring(z, 8, s)], z_in.at[z], z_sems.at[0, 0], z_sems.at[1, 0], zs[s][1], zs[s][0])
    z_in[z] = z_out[z]
    yield
    await_bytes(z_in.at[0:7], z_sems.at[1, 0])
    value = z_in[0].astype(F32)
    for s in range(1, 8):
        value = value + z_in[s].astype(F32)
    z_done[z] = value.astype(BF16)
    for s in (4, 3, 5, 2, 6, 1, 7):
        send(z_done.at[z], z_done.at[z], z_sems.at[0, 1], z_sems.at[1, 1], zs[s][1], zs[s][0])
    yield
    await_bytes(z_done.at[0:7], z_sems.at[1, 1])
    back = {}

    def columns(h):
        return slice(256 * h, 256 * h + 256)

    def share(h, base, axis, size, stage):
        part = total.at[rows_at(base + axis[0] * size, size), columns(h)]
        for s in (2, 1, 3):
            back[stage, h, s] = post(part, part, (stage, h, s), axis[1][s])

    bases = [core * half + chunk(outer[h], 0, large) for h in both]
    for h in both:
        at = bases[h] + chunk(inner[h], 0, small)
        for j in (2 * h, 2 * h + 1):
            joined = jnp.concatenate([z_done[2 * j + k, 0:piece].astype(F32) for k in both], axis=0)
            total[rows_at(at, small), 128 * j : 128 * j + 128] = joined.astype(BF16)
        share(h, bases[h], inner[h], small, 3)
    yield
    for h in both:
        for s in (1, 2, 3):
            back[3, h, s].wait_recv()
        share(h, core * half, outer[h], large, 4)
    last = []

    def to_sibling(h, s):
        part = total.at[rows_at(core * half + chunk(outer[h], -s, large), large), columns(h)]
        last.append(post(part, part, (5, h, s), (x, sibling)))

    for h in both:
        to_sibling(h, 0)
    yield
    for s in (1, 3, 2):
        for h in both:
            back[4, h, s].wait_recv()
            to_sibling(h, s)
    yield
    for copy in last:
        copy.wait_recv()
    await_bytes(z_out.at[0:7], z_sems.at[0, 0])
    await_bytes(z_done.at[0:7], z_sems.at[0, 1])


def gain_reduction(value, result, where, slots, sems):
    x, y, z, core, here, xs, ys, zs = where
    cores = [(x, here), (x, here + 1 - 2 * core)]
    base = 0
    for index, (count, pos, devices) in enumerate(((2, core, cores), (4, x, xs), (4, y, ys), (8, z, zs))):
        slots[base + pos] = value
        for s in range(1, count):
            mine = slots.at[base + pos]
            send(mine, mine, sems.at[0, index], sems.at[1, index], devices[s][1], devices[s][0])
        yield
        await_bytes(slots.at[base : base + count - 1], sems.at[1, index])
        await_bytes(slots.at[base : base + count - 1], sems.at[0, index])
        value = slots[base]
        for s in range(1, count):
            value = value + slots[base + s]
        base += count
    result[...] = value


def advance(step):
    next(step, None)


def layer_kernel(
    nodes_in, send_rows, senders, receivers, gain, ngain, lat_in, cot_in, ncot_in, w1_in, w2_in, nw1_in, nw2_in,
    edge_grad, node_grad, own_total, table_total, node_total, gain_total,
    nodes, lat, cot, ncot, w1, w2, nw1, nw2, others, packed, incoming, far_grad, returned, rim_grad, from_rims,
    onehot, projected, act, slope, hat, scale, raw_grad, pre_grad, node_partial, own_terms, table_terms, node_terms, slots, *rest,
):
    own_scratch, table_scratch, node_scratch = rest[0:10], rest[10:20], rest[20:30]
    load_sems, far_sems, rim_sems, back_sems, back_rim_sems, gain_sems = rest[30:]
    here, x, y, z, core = place()
    edges, width = lat.shape
    count = nodes.shape[0]
    patches = send_rows.shape[1]
    outside = others.shape[0]
    rows = count + outside
    block = 256
    xs = [(x, here)] + [(ring(x, 4, s), here) for s in (1, 2, 3)]
    ys = [(x, here)] + [(x, ring(y, 4, s) * 16 + z * 2 + core) for s in (1, 2, 3)]
    zs = [(x, here)] + [(x, y * 16 + ring(z, 8, s) * 2 + core) for s in range(1, 8)]
    where = (x, y, z, core, here, xs, ys, zs)
    behind, ahead = ring(here, patches, -1), ring(here, patches, 1)

    loads = [
        pltpu.make_async_copy(src, dst, load_sems.at[k])
        for k, (src, dst) in enumerate(
            (
                (nodes_in, nodes), (w1_in, w1), (lat_in, lat), (w2_in, w2),
                (nw1_in, nw1), (nw2_in, nw2), (ncot_in, ncot), (cot_in, cot),
            )
        )
    ]
    for copy in loads:
        copy.start()

    def greet(k, carry):
        signal(lax.rem(here + k, patches), x)
        return carry

    lax.fori_loop(1, patches, greet, 0)
    for s in (1, 2, 3):
        signal(here, ring(x, 4, s))
    spread_nodes = send_one_hot(send_rows[...], count)
    loads[0].wait()
    packed[...] = pack(mm_tn(spread_nodes, nodes[...]).astype(BF16), False)
    pl.semaphore_wait(pltpu.get_barrier_semaphore(), patches + 2)
    rims = (
        send(nodes.at[count - RIM : count], others.at[0:RIM], rim_sems.at[0, 0], rim_sems.at[1, 0], ahead, x),
        send(nodes.at[0:RIM], others.at[RIM : 2 * RIM], rim_sems.at[0, 1], rim_sems.at[1, 1], behind, x),
    )

    def push(src, dst, sems, first, last):
        def one(k, carry):
            row = lax.rem(y + 2 + k // 2, 4) * 16 + lax.rem(core + k, 2)
            for s in (4, 3, 5, 2, 6, 1, 7, 0):
                to = row + ring(z, 8, s) * 2

                def go():
                    send(src.at[rows_at(to * 16, 16)], dst.at[rows_at(here * 16, 16)], sems.at[0], sems.at[1], to, x)

                if s == 0:
                    pl.when(to != here)(go)
                else:
                    go()
            return carry

        lax.fori_loop(first, last, one, 0)

    mine = rows_at(here * 16, 16)
    all_but_mine = slice(0, 16 * (patches - 1))
    push(packed, incoming, far_sems, 0, patches // 8)

    send_row, recv_row = senders[...], receivers[...]
    table_row = jnp.where(send_row < RIM, send_row + count, jnp.where(send_row < RIM + count, send_row - RIM, send_row))
    send_col = jnp.transpose(jnp.broadcast_to(table_row, (128, edges)))
    recv_col = jnp.transpose(jnp.broadcast_to(recv_row, (128, edges)))
    onehot[:, 0:count] = one_hot_cols(send_col, count)
    onehot[:, count : 2 * count] = one_hot_cols(recv_col, count)
    onehot[:, 2 * count : 2 * count + outside] = one_hot_cols(send_col, outside, count)
    recv_rows = one_hot_rows(recv_row, count)
    loads[1].wait()
    projected[0:count, :] = mm(nodes[...], w1[width : 2 * width, :]).astype(BF16)
    projected[count : 2 * count, :] = mm(nodes[...], w1[2 * width :, :]).astype(BF16)
    loads[2].wait()
    for start in range(0, edges, block):
        part = slice(start, start + block)
        slope[part, :] = mm(lat[part, :], w1[0:width, :]) + mm(onehot[part, 0 : 2 * count], projected[0 : 2 * count, :])

    for copy in rims:
        copy.wait_recv()
    incoming[mine, :] = packed[mine, :]
    await_bytes(incoming.at[all_but_mine], far_sems.at[1])
    others[2 * RIM :, :] = unpack(incoming[...], True)
    projected[2 * count : 2 * count + outside, :] = mm(others[...], w1[width : 2 * width, :]).astype(BF16)
    loads[3].wait()
    edge_gain = gain[...]
    inflow = jnp.zeros((count, width), F32)
    for start in range(0, edges, block):
        part = slice(start, start + block)
        pre = slope[part, :] + mm(onehot[part, 2 * count :], projected[2 * count :, :])
        sig = jax.nn.sigmoid(pre)
        acted = (pre * sig).astype(BF16)
        act[part, :] = acted
        slope[part, :] = sig * (1.0 + pre * (1.0 - sig))
        normed, inv = normalize(mm(acted, w2[...]))
        hat[part, :] = normed
        scale[part, :] = inv
        inflow = inflow + mm(recv_rows[:, part], (normed * edge_gain).astype(BF16))
    inflow = inflow.astype(BF16)
    for copy in loads[4:]:
        copy.wait()
    node_pre = mm(nodes[...], nw1[0:width, :]) + mm(inflow, nw1[width:, :])
    node_sig = jax.nn.sigmoid(node_pre)
    node_act = (node_pre * node_sig).astype(BF16)
    node_hat, node_scale = normalize(mm(node_act, nw2[...]))
    upstream = ncot[...].astype(F32)
    node_gain_grad = jnp.sum(upstream * node_hat, axis=0, keepdims=True)
    node_raw_grad = normalize_back(upstream * ngain[...], node_hat, node_scale).astype(BF16)
    node_act_grad = mm_nt(node_raw_grad, nw2[...])
    node_pre_grad = (node_act_grad * node_sig * (1.0 + node_pre * (1.0 - node_sig))).astype(BF16)

    def put(terms, row, value):
        for j in range(width // 128):
            terms[j, row : row + value.shape[0], :] = value[:, 128 * j : 128 * j + 128].astype(BF16)

    put(node_terms, 0, mm_tn(nodes[...], node_pre_grad))
    put(node_terms, width, mm_tn(inflow, node_pre_grad))
    put(node_terms, 2 * width, mm_tn(node_act, node_raw_grad))
    pending = []
    node_sum = reduction(node_terms, node_total, where, node_scratch, pending)
    advance(node_sum)
    inflow_grad = mm_nt(node_pre_grad, nw1[width:, :]).astype(BF16)
    gain_grad = jnp.zeros((1, width), F32)
    for start in range(0, edges, block):
        part = slice(start, start + block)
        edge_cot = cot[part, :].astype(F32)
        normed = hat[part, :]
        update_grad = edge_cot + mm(onehot[part, count : 2 * count], inflow_grad)
        gain_grad = gain_grad + jnp.sum(update_grad * normed, axis=0, keepdims=True)
        back = normalize_back(update_grad * edge_gain, normed, scale[part, :]).astype(BF16)
        raw_grad[part, :] = back
        pre_back = (mm_nt(back, w2[...]) * slope[part, :]).astype(BF16)
        pre_grad[part, :] = pre_back
        if start == 0:
            advance(node_sum)
    all_pre = pre_grad[...]
    put(own_terms, width, mm_tn(act[...], raw_grad[...]))
    put(own_terms, 0, mm_tn(lat[...], all_pre))
    own_sum = reduction(own_terms, own_total, where, own_scratch, pending)
    advance(own_sum)
    send_sum = mm(one_hot_rows(table_row, rows), all_pre).astype(BF16)
    recv_sum = mm(recv_rows, all_pre).astype(BF16)
    put(table_terms, 0, mm_tn(nodes[...], send_sum[0:count]) + mm_tn(others[...], send_sum[count:]))
    put(table_terms, width, mm_tn(nodes[...], recv_sum))
    table_sum = reduction(table_terms, table_total, where, table_scratch, pending)
    advance(table_sum)
    advance(own_sum)
    gain_rows = [gain_grad[:, 128 * j : 128 * j + 128] for j in range(width // 128)]
    gain_rows += [node_gain_grad[:, 128 * j : 128 * j + 128] for j in range(width // 128)]
    gain_sum = gain_reduction(jnp.concatenate(gain_rows, axis=0), gain_total, where, slots, gain_sems)
    advance(gain_sum)
    other_grad = mm_nt(send_sum[count:], w1[width : 2 * width, :]).astype(BF16)
    rim_grad[...] = other_grad[0 : 2 * RIM]
    back_rims = (
        send(rim_grad.at[RIM : 2 * RIM], from_rims.at[0:RIM], back_rim_sems.at[0, 0], back_rim_sems.at[1, 0], ahead, x),
        send(rim_grad.at[0:RIM], from_rims.at[RIM : 2 * RIM], back_rim_sems.at[0, 1], back_rim_sems.at[1, 1], behind, x),
    )
    advance(table_sum)
    advance(node_sum)
    far_grad[...] = pack(other_grad[2 * RIM :], True)
    node_partial[...] = upstream + mm_nt(node_pre_grad, nw1[0:width, :])
    node_partial[...] += mm_nt(send_sum[0:count], w1[width : 2 * width, :]) + mm_nt(recv_sum, w1[2 * width :, :])
    for start in range(0, edges, block):
        part = slice(start, start + block)
        edge_grad[part, :] = (cot[part, :].astype(F32) + mm_nt(pre_grad[part, :], w1[0:width, :])).astype(BF16)
    advance(gain_sum)
    returned[mine, :] = far_grad[mine, :]
    for step in (own_sum, node_sum, table_sum, gain_sum, own_sum, table_sum, node_sum):
        advance(step)
    parts = patches // 8
    turns = (own_sum, table_sum, node_sum, own_sum, table_sum, node_sum, own_sum, table_sum)
    for k, step in enumerate(turns):
        push(far_grad, returned, back_sems, parts * k // 8, parts * (k + 1) // 8)
        advance(step)
        if k == 4:
            advance(gain_sum)
    advance(gain_sum)
    advance(node_sum)
    for copy in back_rims:
        copy.wait_recv()
    await_bytes(returned.at[all_but_mine], back_sems.at[1])
    nodes_done = node_partial[...] + mm(spread_nodes, unpack(returned[...], False))
    node_grad[0:RIM, :] = (nodes_done[0:RIM] + from_rims[0:RIM].astype(F32)).astype(BF16)
    node_grad[RIM : count - RIM, :] = nodes_done[RIM : count - RIM].astype(BF16)
    node_grad[count - RIM : count, :] = (nodes_done[count - RIM :] + from_rims[RIM : 2 * RIM].astype(F32)).astype(BF16)
    for _ in (0, 1):
        advance(own_sum)
        advance(table_sum)
        advance(node_sum)
    for copy in rims + back_rims:
        copy.wait_send()
    await_bytes(packed.at[all_but_mine], far_sems.at[0])
    await_bytes(far_grad.at[all_but_mine], back_sems.at[0])
    for copy in pending:
        copy.wait_send()


def place_kernel(
    own_total, table_total, node_total, edge_in, node_in, gains, first, second, nfirst, nsecond, edge_out, node_out, gain_out, ngain_out, sems
):
    width = first.shape[1]
    copies = [
        pltpu.make_async_copy(src, dst, sems.at[k])
        for k, (src, dst) in enumerate(
            (
                (own_total.at[0:width], first.at[0:width]),
                (table_total, first.at[width : 3 * width]),
                (own_total.at[width : 2 * width], second),
                (node_total.at[0 : 2 * width], nfirst),
                (node_total.at[2 * width : 3 * width], nsecond),
                (edge_in, edge_out),
                (node_in, node_out),
            )
        )
    ]
    for copy in copies:
        copy.start()
    for j in range(width // 128):
        cols = slice(128 * j, 128 * j + 128)
        gain_out[cols] = gains[j, :].astype(BF16)
        ngain_out[cols] = gains[4 + j, :].astype(BF16)
    for copy in copies:
        copy.wait()


def place_results(own_total, table_total, node_total, edge_grad, node_grad, gains):
    width = edge_grad.shape[1]
    anywhere, whole = pl.BlockSpec(memory_space=pl.ANY), pl.BlockSpec(memory_space=VMEM)
    return pl.pallas_call(
        place_kernel,
        out_shape=tuple(
            jax.ShapeDtypeStruct(shape, BF16)
            for shape in (
                (3 * width, width), (width, width), (2 * width, width), (width, width),
                edge_grad.shape, node_grad.shape, (width,), (width,),
            )
        ),
        in_specs=[whole] * 6,
        out_specs=(anywhere,) * 6 + (whole,) * 2,
        scratch_shapes=[pltpu.SemaphoreType.DMA((7,))],
        compiler_params=pltpu.CompilerParams(vmem_limit_bytes=16 * 1024 * 1024),
        name="place_results",
    )(own_total, table_total, node_total, edge_grad, node_grad, gains)


def reduction_scratch(total):
    half = total // 2
    large, small = half // 4, half // 16
    padded = -(-(small // 2) // 16) * 16
    dma = pltpu.SemaphoreType.DMA
    return [
        VMEM((4, half, 128), BF16),
        VMEM((4, half, 128), BF16),
        VMEM((2, 3, 2, large, 128), BF16),
        VMEM((4, large, 128), BF16),
        VMEM((2, 3, 2, small, 128), BF16),
        VMEM((8, padded, 128), BF16),
        VMEM((8, padded, 128), BF16),
        VMEM((8, padded, 128), BF16),
        dma((2, 6, 2, 4)),
        dma((2, 2)),
    ]


def layer(lat, cot, nodes, ncot, senders, receivers, send_rows, w1, w2, gain, nw1, nw2, ngain):
    edges, width = lat.shape
    count = nodes.shape[0]
    patches = send_rows.shape[1]
    outside = 2 * RIM + FAR * patches
    anywhere, whole = pl.BlockSpec(memory_space=pl.ANY), pl.BlockSpec(memory_space=VMEM)
    dma = pltpu.SemaphoreType.DMA
    packed = VMEM((16 * patches, 128), BF16)
    return pl.pallas_call(
        layer_kernel,
        out_shape=(
            VMEM((edges, width), BF16),
            VMEM((count, width), BF16),
            VMEM((2 * width, width), BF16),
            VMEM((2 * width, width), BF16),
            VMEM((3 * width, width), BF16),
            VMEM((8, 128), F32),
        ),
        in_specs=[anywhere] + [whole] * 5 + [anywhere] * 7,
        out_specs=(whole,) * 6,
        scratch_shapes=[
            VMEM(nodes.shape, BF16),
            VMEM(lat.shape, BF16),
            VMEM(cot.shape, BF16),
            VMEM(ncot.shape, BF16),
            VMEM(w1.shape, BF16),
            VMEM(w2.shape, BF16),
            VMEM(nw1.shape, BF16),
            VMEM(nw2.shape, BF16),
            VMEM((outside, width), BF16),
            packed,
            packed,
            packed,
            packed,
            VMEM((2 * RIM, width), BF16),
            VMEM((2 * RIM, width), BF16),
            VMEM((edges, 2 * count + outside), BF16),
            VMEM((2 * count + outside, width), BF16),
            VMEM((edges, width), BF16),
            VMEM((edges, width), F32),
            VMEM((edges, width), F32),
            VMEM((edges, 1), F32),
            VMEM((edges, width), BF16),
            VMEM((edges, width), BF16),
            VMEM((count, width), F32),
            VMEM((4, 2 * width, 128), BF16),
            VMEM((4, 2 * width, 128), BF16),
            VMEM((4, 3 * width, 128), BF16),
            VMEM((18, 8, 128), F32),
        ]
        + reduction_scratch(2 * width)
        + reduction_scratch(2 * width)
        + reduction_scratch(3 * width)
        + [dma((8,)), dma((2,)), dma((2, 2)), dma((2,)), dma((2, 2)), dma((2, 4))],
        compiler_params=pltpu.CompilerParams(
            collective_id=0, has_side_effects=True, vmem_limit_bytes=56 * 1024 * 1024
        ),
        name="layer",
    )(
        nodes, send_rows, senders.reshape(1, edges), receivers.reshape(1, edges),
        gain.reshape(1, width), ngain.reshape(1, width), lat, cot, ncot, w1, w2, nw1, nw2,
    )


def on_device(
    edge_latents, node_latents, edge_cotangent, node_cotangent, senders, receivers, send_rows,
    edge_first, edge_second, edge_gain, node_first, node_second, node_gain,
):
    width = edge_first.shape[1]
    edge_grad, node_grad, own_total, table_total, node_total, gains = layer(
        edge_latents[0], edge_cotangent[0], node_latents[0], node_cotangent[0], senders, receivers, send_rows.T,
        edge_first, edge_second, edge_gain, node_first, node_second, node_gain,
    )
    first, second, nfirst, nsecond, edge_grad, node_grad, gain_grad, ngain_grad = place_results(
        own_total, table_total, node_total, edge_grad, node_grad, gains
    )
    return (
        edge_grad[None], node_grad[None], first, second, nfirst, nsecond,
        gain_grad, ngain_grad,
    )


def solution(mesh):
    return jax.shard_map(
        on_device,
        mesh=mesh,
        in_specs=(
            P("sample", "patch", None), P("sample", "patch", None), P("sample", "patch", None),
            P("sample", "patch", None), P("patch"), P("patch"), P("patch", None),
            P(), P(), P(), P(), P(), P(),
        ),
        out_specs=(P("sample", "patch", None), P("sample", "patch", None), P(), P(), P(), P(), P(), P()),
        check_vma=False,
    )
```
